128 devices in a mesh: grp: 8 (over z, core), dev: 16 (over y, x).
Axes of the slice: x: 4, y: 4, z: 4, core: 2. Of those that a mesh axis runs over, the one named last changes fastest.
Arguments:
- coarse_state: float32 [9, 128, 128, 128], P(None, 'grp', 'dev'), may hold values from -6 to 6
- coef_index: int32 [128, 128, 128], P('grp', 'dev'), may hold values from 0 to 7
- coef_table: float32 [8, 9], replicated, may hold values from 0.05 to 1
- patch_root: int32 [128, 3], replicated, may hold values from 0 to 112, as said below
- fine_index: int32 [128, 32, 1024], P(('grp', 'dev')), may hold values from 0 to 7
Outputs:
- coarse_new: float32 [9, 128, 128, 128], P(None, 'grp', 'dev')
- fine_state: float32 [128, 9, 32, 1024], P(('grp', 'dev'))
The draws below stay inside these ranges and needn't reach their ends.
Inputs may be any that keep to these rules, and one draw needn't show every extreme that they name: `patch_root`: row i is patch number k = i % 1 of device (i % 16) // 1 of group i // 16. Its first coordinate lies from (i // 16) * 16 to (i // 16) * 16 + 16 - 16; with q = 128, its second lies from k * q + 1 to k * q + q - 17; its third from 1 to 111. Patches may intersect; their corrections add.
All inputs are finite; a program needn't handle non-finite values.
Results may differ from the reference program's by a relative error of at most 0.0003.
Values sent between devices are 32-bit elements; how exact they have to be, the bound alone decides.
No kernel may reach another device: no remote copies, remote signals or barrier semaphores. Data moves between devices by JAX's collectives and lax.ppermute only.
A program may use at most 192 MiB of HBM per device.

```python
import math
import jax
import jax.numpy as jnp
from jax import lax

S = 9
B = 16
K = 8
NSUB = 2
CX = 16
PATCH_DEV = 1
NX = 128
NY = 128
NZ = 128
PG = 16
NP = 128


def draw_patch_root(key, part):
    key = jax.random.fold_in(key, 7)
    keys = jax.random.split(key, 3)
    rows = jnp.arange(NP, dtype=jnp.int32)
    group = rows // PG
    within = rows % PATCH_DEV
    stripe = NY // PATCH_DEV
    first = group * CX + jax.random.randint(keys[0], (NP,), 0, CX - B + 1, dtype=jnp.int32)
    second = within * stripe + 1 + jax.random.randint(keys[1], (NP,), 0, stripe - B - 1, dtype=jnp.int32)
    third = jax.random.randint(keys[2], (NP,), 1, NZ - B, dtype=jnp.int32)
    first = jnp.where(rows == 0, 0, jnp.where(rows == NP - 1, NX - B, first))
    second = jnp.where(rows == 0, 1, jnp.where(rows == NP - 1, NY - B - 1, second))
    third = jnp.where(rows == 0, 1, jnp.where(rows == NP - 1, NZ - B - 1, third))
    return jnp.stack([first, second, third], axis=1).astype(jnp.int32)


def touch_ends(values, key, low, top_value):
    longest = values.shape.index(max(values.shape))
    spots = []
    for shift in (0, 1):
        where = [jax.random.randint(jax.random.fold_in(key, axis), (), 0, length) for axis, length in enumerate(values.shape)]
        where[longest] = (where[longest] + shift) % values.shape[longest]
        spots.append(tuple(where))
    return values.at[spots[0]].set(low).at[spots[1]].set(top_value)


def levels(rng, dims, pieces, smallest, high):
    level, own = 1.0, jax.random.fold_in(rng, 6)
    for axis_at, blocks in pieces:
        heights = jnp.exp(jax.random.uniform(jax.random.fold_in(own, axis_at), (blocks,), jnp.float32, smallest / len(pieces), high / len(pieces)))
        level = level * jnp.repeat(heights, dims[axis_at] // blocks).reshape([-1 if axis == axis_at else 1 for axis in range(len(dims))])
    return level


def noise(key, dims, scale, reach, pieces=(), kind=jnp.bfloat16):
    values = scale * jax.random.normal(key, dims, jnp.float32)
    if pieces:
        values = values * levels(key, dims, pieces, -0.22, 0.18)
    return jnp.clip(values, -reach, reach).astype(kind)


def setup_inputs(seed: int = 0) -> dict:
    seeds = jax.random.split(jax.random.key(seed), 6)
    coarse_state = noise(seeds[0], (S, NX, NY, NZ), 1.0, 6.0, ((1, 8), (2, 16)), jnp.float32)
    coef_index = touch_ends(jax.random.randint(seeds[1], (NX, NY, NZ), 0, K), jax.random.fold_in(seeds[1], 1), 0, K - 1).astype(jnp.int32)
    coef_table = jnp.clip(jnp.exp(jax.random.uniform(seeds[2], (K, S), jnp.float32, math.log(0.05), math.log(1.0))), 0.05, 1.0)
    patch_root = draw_patch_root(jax.random.fold_in(seeds[5], 71), 0)
    fine_index = touch_ends(jax.random.randint(seeds[4], (NP, 2 * B, 4 * B * B), 0, K), jax.random.fold_in(seeds[4], 1), 0, K - 1).astype(jnp.int32)
    return dict(coarse_state=coarse_state, coef_index=coef_index, coef_table=coef_table, patch_root=patch_root, fine_index=fine_index)


lam_coarse = 0.08
lam_fine = 0.16


def lookup(index_field, table):
    result = jnp.zeros((table.shape[1],) + index_field.shape, jnp.float32)
    for category in range(table.shape[0]):
        result = result + jnp.where(index_field[None] == category, table[category].reshape((-1, 1, 1, 1)), jnp.float32(0.0))
    return result


def coarse_step(field, diff):
    center = field[:, 1:-1, 1:-1, 1:-1]
    dcenter = diff[:, 1:-1, 1:-1, 1:-1]

    def term(nbr_u, nbr_d):
        return 0.5 * (dcenter + nbr_d) * (nbr_u - center)

    total = term(field[:, :-2, 1:-1, 1:-1], diff[:, :-2, 1:-1, 1:-1])
    total = total + term(field[:, 2:, 1:-1, 1:-1], diff[:, 2:, 1:-1, 1:-1])
    total = total + term(field[:, 1:-1, :-2, 1:-1], diff[:, 1:-1, :-2, 1:-1])
    total = total + term(field[:, 1:-1, 2:, 1:-1], diff[:, 1:-1, 2:, 1:-1])
    total = total + term(field[:, 1:-1, 1:-1, :-2], diff[:, 1:-1, 1:-1, :-2])
    total = total + term(field[:, 1:-1, 1:-1, 2:], diff[:, 1:-1, 1:-1, 2:])
    return center + lam_coarse * total


def upsample(block):
    return jnp.repeat(jnp.repeat(jnp.repeat(block, 2, 1), 2, 2), 2, 3)


def ghost_fill(coarse):
    return upsample(coarse)[:, 1:-1, 1:-1, 1:-1]


def prolong(coarse):
    side = coarse.shape[1] - 2
    inner = slice(1, side + 1)
    core = coarse[:, inner, inner, inner]
    slope_x = (coarse[:, 2:, inner, inner] - coarse[:, :-2, inner, inner]) * 0.125
    slope_y = (coarse[:, inner, 2:, inner] - coarse[:, inner, :-2, inner]) * 0.125
    slope_z = (coarse[:, inner, inner, 2:] - coarse[:, inner, inner, :-2]) * 0.125
    signs = jnp.tile(jnp.array([-1.0, 1.0], jnp.float32), side)
    interior = upsample(core) + signs.reshape((1, -1, 1, 1)) * upsample(slope_x)
    interior = interior + signs.reshape((1, 1, -1, 1)) * upsample(slope_y)
    interior = interior + signs.reshape((1, 1, 1, -1)) * upsample(slope_z)
    return ghost_fill(coarse).at[:, 1:-1, 1:-1, 1:-1].set(interior)


def coarsen_face(register):
    species, fine_n, _ = register.shape
    return register.reshape((species, fine_n // 2, 2, fine_n // 2, 2)).sum(axis=(2, 4))


def patch_work(foot_u, foot_d, fine_idx, table):
    side = foot_u.shape[1] - 2
    fine_n = 2 * side
    species = foot_u.shape[0]
    field = prolong(foot_u)
    dext = ghost_fill(foot_d).at[:, 1:-1, 1:-1, 1:-1].set(lookup(fine_idx, table))
    zero_face = jnp.zeros((species, fine_n, fine_n), jnp.float32)
    regs = [zero_face] * 6
    for substep in range(NSUB):
        core = field[:, 1:-1, 1:-1, 1:-1]
        flux_x = 0.5 * (dext[:, 1:, 1:-1, 1:-1] + dext[:, :-1, 1:-1, 1:-1]) * (field[:, 1:, 1:-1, 1:-1] - field[:, :-1, 1:-1, 1:-1])
        flux_y = 0.5 * (dext[:, 1:-1, 1:, 1:-1] + dext[:, 1:-1, :-1, 1:-1]) * (field[:, 1:-1, 1:, 1:-1] - field[:, 1:-1, :-1, 1:-1])
        flux_z = 0.5 * (dext[:, 1:-1, 1:-1, 1:] + dext[:, 1:-1, 1:-1, :-1]) * (field[:, 1:-1, 1:-1, 1:] - field[:, 1:-1, 1:-1, :-1])
        change = (flux_x[:, 1:] - flux_x[:, :-1]) + (flux_y[:, :, 1:] - flux_y[:, :, :-1])
        change = change + (flux_z[:, :, :, 1:] - flux_z[:, :, :, :-1])
        field = field.at[:, 1:-1, 1:-1, 1:-1].set(core + lam_fine * change)
        regs = [regs[0] + flux_x[:, 0], regs[1] - flux_x[:, fine_n],
                regs[2] + flux_y[:, :, 0], regs[3] - flux_y[:, :, fine_n],
                regs[4] + flux_z[:, :, :, 0], regs[5] - flux_z[:, :, :, fine_n]]
    inner = slice(1, side + 1)
    last = side + 1

    def face_flux(cycle_u, cycle_d, edge_u, edge_d):
        return lam_coarse * (0.5 * (cycle_d + edge_d)) * (edge_u - cycle_u)

    coarse_faces = [
        face_flux(foot_u[:, 0, inner, inner], foot_d[:, 0, inner, inner], foot_u[:, 1, inner, inner], foot_d[:, 1, inner, inner]),
        face_flux(foot_u[:, last, inner, inner], foot_d[:, last, inner, inner], foot_u[:, side, inner, inner], foot_d[:, side, inner, inner]),
        face_flux(foot_u[:, inner, 0, inner], foot_d[:, inner, 0, inner], foot_u[:, inner, 1, inner], foot_d[:, inner, 1, inner]),
        face_flux(foot_u[:, inner, last, inner], foot_d[:, inner, last, inner], foot_u[:, inner, side, inner], foot_d[:, inner, side, inner]),
        face_flux(foot_u[:, inner, inner, 0], foot_d[:, inner, inner, 0], foot_u[:, inner, inner, 1], foot_d[:, inner, inner, 1]),
        face_flux(foot_u[:, inner, inner, last], foot_d[:, inner, inner, last], foot_u[:, inner, inner, side], foot_d[:, inner, inner, side]),
    ]
    corrections = [(lam_fine * 0.125) * coarsen_face(regs[number]) - coarse_faces[number] for number in range(6)]
    interior = field[:, 1:-1, 1:-1, 1:-1]
    means = interior.reshape((species, side, 2, side, 2, side, 2)).sum(axis=(2, 4, 6)) * 0.125
    delta = jnp.zeros(foot_u.shape, jnp.float32)
    delta = delta.at[:, inner, inner, inner].set(means - coarse_step(foot_u, foot_d))
    delta = delta.at[:, 0, inner, inner].set(corrections[0])
    delta = delta.at[:, last, inner, inner].set(corrections[1])
    delta = delta.at[:, inner, 0, inner].set(corrections[2])
    delta = delta.at[:, inner, last, inner].set(corrections[3])
    delta = delta.at[:, inner, inner, 0].set(corrections[4])
    delta = delta.at[:, inner, inner, last].set(corrections[5])
    return interior, delta


def reference(coarse_state, coef_index, coef_table, patch_root, fine_index):
    padded_u = jnp.pad(coarse_state, ((0, 0), (1, 1), (1, 1), (1, 1)))
    padded_idx = jnp.pad(coef_index, ((1, 1), (1, 1), (1, 1)), constant_values=-1)

    def species_step(inputs):
        field, column = inputs
        diff = lookup(padded_idx, column.reshape((-1, 1)))
        return coarse_step(field[None], diff)[0]

    coarse_one = lax.map(species_step, (padded_u, coef_table.T))
    width = B + 2
    fine_n = 2 * B

    def patch_scan(totals, inputs):
        root, fine_idx = inputs
        start_x, start_y, start_z = root[0], root[1], root[2]
        foot_u = lax.dynamic_slice(padded_u, (jnp.int32(0), start_x, start_y, start_z), (S, width, width, width))
        foot_i = lax.dynamic_slice(padded_idx, (start_x, start_y, start_z), (width, width, width))
        foot_d = lookup(foot_i, coef_table)
        interior, delta = patch_work(foot_u, foot_d, fine_idx.reshape((fine_n, fine_n, fine_n)), coef_table)
        anchor = (jnp.int32(0), start_x, start_y, start_z)
        current = lax.dynamic_slice(totals, anchor, (S, width, width, width))
        totals = lax.dynamic_update_slice(totals, current + delta, anchor)
        return totals, interior

    zero_total = jnp.zeros(padded_u.shape, jnp.float32)
    totals, fines = lax.scan(patch_scan, zero_total, (patch_root.astype(jnp.int32), fine_index))
    coarse_new = coarse_one + totals[:, 1:-1, 1:-1, 1:-1]
    fine_state = fines.reshape((NP, S, fine_n, fine_n * fine_n))
    return coarse_new, fine_state
```

```python
import jax
import jax.numpy as jnp
import ml_dtypes
import numpy as np
from jax import lax
from jax.experimental import pallas as pl
from jax.experimental.pallas import tpu as pltpu
from jax.sharding import PartitionSpec as P

F32 = jnp.float32
S = 9
CH = 10
CX = 16
CY = 8
DEV = 16
W = 18
PITCH = 24
FRAME = W * W
BLK = CY * W
SLAB_ROWS = CH * CX + 2 * CH
GF = 23
NF = GF + 3
TR = GF * 8
GB = 21
NB = GB + 3
CLS = 9
VMEM = pl.BlockSpec(memory_space=pltpu.VMEM)
SMEM = pl.BlockSpec(memory_space=pltpu.SMEM)


def weights():
    wf = np.zeros((128, 384), np.float32)
    rb = np.zeros((2, 128, 128), np.float32)
    for lane in range(128):
        q, fz = divmod(lane, 32)
        k, z = 1 + q // 2, fz // 2 + 1
        sy, sz = (0.125 if q % 2 else -0.125), (0.125 if fz % 2 else -0.125)
        wf[k * W + z, lane] += 1.0
        wf[(k + 1) * W + z, lane] += sy
        wf[(k - 1) * W + z, lane] -= sy
        wf[k * W + z + 1, lane] += sz
        wf[k * W + z - 1, lane] -= sz
        wf[k * W + z, 256 + lane] = 1.0
        rb[0, lane, (q // 2) * W + z] = 0.125
        if fz == 0:
            wf[k * W, 128 + lane] = 1.0
            rb[1, lane, (q // 2) * W] = 0.125
        if fz == 31:
            wf[k * W + W - 1, 128 + lane] = 1.0
            rb[1, lane, (q // 2) * W + W - 1] = 0.125
    wy = np.zeros((128, 128), np.float32)
    ry = np.zeros((128, 128), np.float32)
    for fz in range(32):
        z = fz // 2 + 1
        wy[z, fz] = 1.0
        wy[W + z, 96 + fz] = 1.0
        ry[fz, z] = 0.125
        ry[96 + fz, 50 + z] = 0.125
    twice = lambda m: np.concatenate([m, m], 0).astype(ml_dtypes.bfloat16)
    return twice(wf), twice(wy), np.concatenate([twice(rb[0]), twice(rb[1])], 0), twice(ry)


def lanes(shape):
    return lax.broadcasted_iota(jnp.int32, shape, 1)


def mod128(x):
    return lax.bitwise_and(x, 127)


def halves(x):
    hi = x.astype(jnp.bfloat16)
    return hi, (x - hi.astype(F32)).astype(jnp.bfloat16)


def pick(tab, index):
    rows = index.shape[0]
    parts = [
        jnp.take_along_axis(tab, index[r : r + 8], axis=1, mode="promise_in_bounds") for r in range(0, rows, 8)
    ]
    return parts[0] if len(parts) == 1 else jnp.concatenate(parts, 0)


def where_is(roots, row):
    first = roots[row, 1] - 1
    owner = lax.shift_right_logical(first, 3)
    return owner, first - 8 * owner, roots[row, 2] - 1


def pack_kernel(roots, u, idx, lo, hi, out, slab):
    grp, me = lax.axis_index("grp"), lax.axis_index("dev")
    for x in range(CX):
        for s in range(S):
            slab[pl.ds(s * CX + x, 8, stride=TR), :] = u[s, x]
        slab[pl.ds(S * CX + x, 8, stride=TR), :] = (idx[x] + 1).astype(F32)
    for c in range(CH):
        slab[pl.ds(CH * CX + c, 8, stride=TR), :] = lo[c]
        slab[pl.ds(CH * CX + CH + c, 8, stride=TR), :] = hi[c]
    for r in range(SLAB_ROWS, TR):
        slab[pl.ds(r, 8, stride=TR), :] = jnp.zeros((8, 128), F32)
    lane = lanes((8, 128))

    def one(p, carry):
        owner, y0, z0 = where_is(roots, grp * DEV + p)

        @pl.when(jnp.logical_and(me >= owner, 8 * (me - owner) - y0 < W))
        def _():
            rest = None
            for g in range(GF):
                main = None
                for y in range(8):
                    rows = slab[y * TR + 8 * g : y * TR + 8 * g + 8, :]
                    moved = pltpu.roll(rows, mod128(W * y + 128 - z0), 1)
                    main = moved if y == 0 else jnp.where(lane >= W * y, moved, main)
                out[p, g] = main
                slot = 16 * (g % 8)
                moved = pltpu.roll(rows, mod128(126 + slot + 128 - z0), 1)
                rest = moved if slot == 0 else jnp.where(lane >= slot, moved, rest)
                if slot == 112 or g == GF - 1:
                    out[p, GF + g // 8] = rest

        return carry

    lax.fori_loop(0, DEV, one, 0)


def coarse_kernel(u, idx, lo, hi, ylo, yhi, ptab, out, cls, px, pyl, pyh, pzl, pzh):
    lane = lanes((8, 128))
    sub = lax.broadcasted_iota(jnp.int32, (8, 128), 0)
    cls[0] = lo[S].astype(jnp.int32)
    cls[CX + 1] = hi[S].astype(jnp.int32)
    for x in range(CX):
        cls[x + 1] = idx[x] + 1

    def below_y(a, row):
        return jnp.where(sub == 0, jnp.broadcast_to(row, (8, 128)), pltpu.roll(a, 1, 0))

    def above_y(a, row):
        return jnp.where(sub == 7, jnp.broadcast_to(row, (8, 128)), pltpu.roll(a, 7, 0))

    def below_z(a):
        return jnp.where(lane == 0, jnp.zeros_like(a), pltpu.roll(a, 1, 1))

    def above_z(a):
        return jnp.where(lane == 127, jnp.zeros_like(a), pltpu.roll(a, 127, 1))

    for x in range(CX + 1):
        px[x] = cls[x + 1] * CLS + cls[x]
    for x in range(CX):
        c = cls[x + 1]
        pyl[x] = c * CLS + below_y(c, ylo[S, x : x + 1, :].astype(jnp.int32))
        pyh[x] = c * CLS + above_y(c, yhi[S, x : x + 1, :].astype(jnp.int32))
        pzl[x] = c * CLS + below_z(c)
        pzh[x] = c * CLS + above_z(c)

    def species(s, carry):
        tab = jnp.broadcast_to(0.5 * ptab[pl.ds(s, 1), :], (8, 128))
        center = u[s, 0]
        flux = pick(tab, px[0]) * (center - lo[s])
        for x in range(CX):
            after = u[s, x + 1] if x + 1 < CX else hi[s]
            next_flux = pick(tab, px[x + 1]) * (after - center)
            total = next_flux - flux
            total = total + pick(tab, pyl[x]) * (below_y(center, ylo[s, x : x + 1, :]) - center)
            total = total + pick(tab, pyh[x]) * (above_y(center, yhi[s, x : x + 1, :]) - center)
            total = total + pick(tab, pzl[x]) * (below_z(center) - center)
            total = total + pick(tab, pzh[x]) * (above_z(center) - center)
            out[s, x] = center + total
            center, flux = after, next_flux
        return carry

    lax.fori_loop(0, S, species, 0)


def patch_kernel(
    roots, recv, fidx, ptab, wf, wy, rb, ry,
    fine, back,
    fr, up, upy, ei, ipx, ipy, ipz, ipb, ua, ub, uy, zg, fx, fy, fz, fb, zr, yr, b1, b2, by, dl, hb,
):
    grp, me = lax.axis_index("grp"), lax.axis_index("dev")
    owner, y0, _ = where_is(roots, grp * DEV + me)
    lane = lanes((8, 128))
    lane_all = lanes((CH * PITCH, 128))
    start = [BLK * k - W * y0 for k in range(4)]
    source = [jnp.minimum(owner + k, DEV - 1) for k in range(4)]
    zero8 = jnp.zeros((8, 128), F32)

    for c in range(CH):
        for t in range(3):
            fr[t, c, 16:24] = zero8
    for g in range(GF):
        slot = 16 * (g % 8)
        main = [pltpu.roll(recv[source[k], g], mod128(start[k] + 256), 1) for k in range(4)]
        rest = [pltpu.roll(recv[source[k], GF + g // 8], mod128(start[k] + 384 - slot), 1) for k in range(3)]

        def over(t, piece, at, below):
            return jnp.where(lane >= at - 128 * t, piece, below)

        tile0 = over(0, main[1], start[1], over(0, rest[0], start[0] + 128, main[0]))
        tile1 = over(1, main[1], start[1], rest[0])
        tile1 = over(1, main[2], start[2], over(1, rest[1], start[1] + 128, tile1))
        tile2 = over(2, main[2], start[2], over(2, rest[1], start[1] + 128, main[1]))
        tile2 = over(2, main[3], start[3], over(2, rest[2], start[2] + 128, tile2))
        tile2 = jnp.where(lane < FRAME - 256, tile2, 0.0)
        for t, tile in enumerate((tile0, tile1, tile2)):
            if g < 2 * CH:
                fr[t, g // 2, 1 + 8 * (g % 2) : 9 + 8 * (g % 2)] = tile
            else:
                for i in range(8):
                    q = 8 * (g - 2 * CH) + i
                    if q < 2 * CH:
                        at = 0 if q < CH else W - 1
                        fr[t, q % CH, at : at + 1] = tile[i : i + 1]

    def spread(values, weight):
        hi, lo = halves(values)
        return jnp.dot(jnp.concatenate([hi, lo], 1), weight, preferred_element_type=F32)

    for j in range(8):
        t, off = divmod(2 * W * j, 128)
        values = fr[t].reshape(CH * PITCH, 128)
        if off:
            values = pltpu.roll(values, 128 - off, 1)
            if off + 4 * W > 128:
                after = pltpu.roll(fr[t + 1].reshape(CH * PITCH, 128), 128 - off, 1)
                values = jnp.where(lane_all < 128 - off, values, after)
        result = spread(values, wf[...])
        for b in range(3):
            up[3 * j + b] = result[:, 128 * b : 128 * b + 128].reshape(CH, PITCH, 128)
    ends = jnp.where(
        lane_all < W,
        pltpu.roll(fr[2].reshape(CH * PITCH, 128), 78, 1),
        pltpu.roll(fr[0].reshape(CH * PITCH, 128), W, 1),
    )
    upy[...] = spread(ends, wy[...]).reshape(CH, PITCH, 128)

    def both(ref_at, values):
        ref_at(0)(values)
        ref_at(1)(values)

    def ghosts(channel):
        for j in range(8):
            values = up[3 * j + 1, channel, 1 : CX + 1]
            zg[j, pl.ds(0, CX, stride=2), :] = values
            zg[j, pl.ds(1, CX, stride=2), :] = values
        values = upy[channel, 1 : CX + 1]
        uy[pl.ds(0, CX, stride=2), :] = values
        uy[pl.ds(1, CX, stride=2), :] = values

    lane32 = lanes((32, 128))
    first_z = lax.bitwise_and(lane32, 31) == 0
    ghosts(S)
    for j in range(8):
        ei[j, 40:48] = jnp.zeros((8, 128), jnp.int32)
        ei[j, 8:40] = fidx[0, :, 128 * j : 128 * j + 128] + 1
        ei[j, 7:8] = up[3 * j + 2, S, 0:1].astype(jnp.int32)
        ei[j, 40:41] = up[3 * j + 2, S, W - 1 : W].astype(jnp.int32)
    y_ghost = uy[...].astype(jnp.int32)
    before = pltpu.roll(y_ghost, 32, 1)
    for j in range(8):
        ipx[j] = ei[j, 8:48] * CLS + ei[j, 7:47]
        c = ei[j, 8:40]
        moved = pltpu.roll(c, 32, 1)
        ipy[j] = c * CLS + jnp.where(lane32 < 32, before, moved)
        before = moved
        z_ghost = zg[j].astype(jnp.int32)
        ipz[j] = c * CLS + jnp.where(first_z, z_ghost, pltpu.roll(c, 1, 1))
        ipb[j] = c * CLS + z_ghost
    ipy[8] = y_ghost * CLS + jnp.where(lane32 < 32, before, pltpu.roll(y_ghost, 32, 1))

    for c in range(CH):
        for j in range(8):
            b1[j, c, 16:24] = zero8
            b2[j, c, 0:8] = zero8
            b2[j, c, 16:24] = zero8
            if c == S:
                b1[j, c, 0:8] = zero8
                b1[j, c, 8:16] = zero8
                b2[j, c, 8:16] = zero8
        by[c, 0:8] = zero8
        by[c, 16:24] = zero8
        if c == S:
            by[c, 8:16] = zero8

    z_low = lax.bitwise_and(lane, 31) == 0
    z_top = lax.bitwise_and(lane, 31) == 31
    y_wrap = lane < 32
    y_keep = lane < 96

    def subcycle(s, src, dst, last):
        for b in range(4):
            rows = slice(8 + 8 * b, 16 + 8 * b)
            own = slice(8 * b, 8 * b + 8)
            u = [src[j, rows] for j in range(8)]
            edge = uy[own]
            moved = [pltpu.roll(a, 32, 1) for a in u]
            moved_edge = pltpu.roll(edge, 32, 1)
            gy = []
            for j in range(8):
                under = jnp.where(y_wrap, moved[j - 1] if j else moved_edge, moved[j])
                gy.append(fy[j, own] * (u[j] - under))
            gy.append(fy[8, own] * (edge - jnp.where(y_wrap, moved[7], moved_edge)))
            shifted = [pltpu.roll(a, 96, 1) for a in gy]
            reg_y = jnp.where(y_wrap, gy[0], jnp.where(y_keep, 0.0, -shifted[8]))
            yr[own] = yr[own] + reg_y if last else reg_y
            for j in range(8):
                change = jnp.where(y_keep, shifted[j], shifted[j + 1]) - gy[j]
                ghost = zg[j, own]
                gz = fz[j, own] * (u[j] - jnp.where(z_low, ghost, pltpu.roll(u[j], 1, 1)))
                gb = fb[j, own] * (ghost - u[j])
                change = change + (jnp.where(z_top, gb, pltpu.roll(gz, 127, 1)) - gz)
                reg_z = jnp.where(z_low, gz, jnp.where(z_top, -gb, 0.0))
                zr[j, own] = zr[j, own] + reg_z if last else reg_z
                low = fx[j, own] * (u[j] - src[j, 7 + 8 * b : 15 + 8 * b])
                top = fx[j, 1 + 8 * b : 9 + 8 * b] * (src[j, 9 + 8 * b : 17 + 8 * b] - u[j])
                change = change + (top - low)
                if b == 0:
                    b1[j, s, 0:1] = b1[j, s, 0:1] + low[0:1] if last else low[0:1]
                if b == 3:
                    b1[j, s, W - 1 : W] = b1[j, s, W - 1 : W] - top[7:8] if last else -top[7:8]
                value = u[j] + change
                dst[j, rows] = value
                if last:
                    fine[0, s, own, 128 * j : 128 * j + 128] = value

    def species(s, carry):
        tab = jnp.broadcast_to(ptab[pl.ds(s, 1), :], (8, 128))
        ghosts(s)
        for j in range(8):
            core = up[3 * j + 2, s]
            slope = 0.125 * (up[3 * j + 2, s, 2 : CX + 2] - up[3 * j + 2, s, 0:CX])
            middle = up[3 * j, s, 1 : CX + 1]
            ua[j, pl.ds(8, CX, stride=2), :] = middle - slope
            ua[j, pl.ds(9, CX, stride=2), :] = middle + slope
            for ref in (ua, ub):
                ref[j, 7:8] = core[0:1]
                ref[j, 40:41] = core[W - 1 : W]
            fx[j] = pick(tab, ipx[j])
            fy[j] = pick(tab, ipy[j])
            fz[j] = pick(tab, ipz[j])
            fb[j] = pick(tab, ipb[j])
        fy[8] = pick(tab, ipy[8])
        subcycle(s, ua, ub, False)
        subcycle(s, ub, ua, True)
        for j in range(8):
            b1[j, s, 1 : CX + 1] = ua[j, pl.ds(8, CX, stride=2), :] + ua[j, pl.ds(9, CX, stride=2), :]
            b2[j, s, 1 : CX + 1] = zr[j, pl.ds(0, CX, stride=2), :] + zr[j, pl.ds(1, CX, stride=2), :]
        by[s, 1 : CX + 1] = yr[pl.ds(0, CX, stride=2), :] + yr[pl.ds(1, CX, stride=2), :]
        return carry

    lax.fori_loop(0, S, species, 0)

    delta = [jnp.zeros((CH * PITCH, 128), F32) for _ in range(3)]
    for j in range(8):
        t, off = divmod(2 * W * j + W, 128)
        parts = halves(b1[j].reshape(CH * PITCH, 128)) + halves(b2[j].reshape(CH * PITCH, 128))
        sums = pltpu.roll(jnp.dot(jnp.concatenate(parts, 1), rb[...], preferred_element_type=F32), off, 1)
        if off + 2 * W > 128:
            dl[t] = (delta[t] + jnp.where(lane_all >= off, sums, 0.0)).reshape(CH, PITCH, 128)
            delta[t] = dl[t].reshape(CH * PITCH, 128)
            delta[t + 1] = delta[t + 1] + jnp.where(lane_all < off, sums, 0.0)
        else:
            delta[t] = delta[t] + sums
    sums = spread(by[...].reshape(CH * PITCH, 128), ry[...])
    delta[0] = delta[0] + jnp.where(lane_all < W, sums, 0.0)
    delta[2] = delta[2] + jnp.where(lane_all >= 50, sums, 0.0)
    for t in range(3):
        dl[t] = delta[t].reshape(CH, PITCH, 128)

    lane24 = lanes((PITCH, 128))
    row24 = lax.broadcasted_iota(jnp.int32, (PITCH, 128), 0)

    def within(a, top):
        return jnp.logical_and(a >= 1, a <= top)

    def shifted_down(tiles, by_lanes):
        moved = [pltpu.roll(a, by_lanes, 1) for a in tiles]
        return [jnp.where(lane24 < by_lanes, moved[t - 1], moved[t]) for t in range(3)]

    def shifted_up(tiles, by_lanes):
        moved = [pltpu.roll(a, 128 - by_lanes, 1) for a in tiles]
        return [jnp.where(lane24 < 128 - by_lanes, moved[t], moved[(t + 1) % 3]) for t in range(3)]

    cells = [fr[t, S].astype(jnp.int32) for t in range(3)]
    for t, (down_y, down_z) in enumerate(zip(shifted_down(cells, W), shifted_down(cells, 1))):
        ipx[t, 0:24] = cells[t] * CLS + pltpu.roll(cells[t], 1, 0)
        ipy[t, 0:24] = cells[t] * CLS + down_y
        ipz[t, 0:24] = cells[t] * CLS + down_z
        cell = lane24 + 128 * t
        y = lax.shift_right_logical(cell * 3641, 16)
        z = cell - W * y
        inside = [within(row24, CX), within(y, CX), within(z, CX)]
        both_in = lambda a, b, c: jnp.logical_and(a, jnp.logical_and(b, c))
        fx[t, 0:24] = jnp.where(both_in(within(row24, CX + 1), inside[1], inside[2]), 0.5, 0.0)
        fy[t, 0:24] = jnp.where(both_in(inside[0], within(y, CX + 1), inside[2]), 0.5, 0.0)
        fz[t, 0:24] = jnp.where(both_in(inside[0], inside[1], within(z, CX + 1)), 0.5, 0.0)
        fb[t, 0:24] = jnp.where(both_in(*inside), 1.0, 0.0)

    def coarse(s, carry):
        tab = jnp.broadcast_to(ptab[pl.ds(s, 1), :], (8, 128))
        u = [fr[t, s] for t in range(3)]
        down_y, down_z = shifted_down(u, W), shifted_down(u, 1)
        gx = [fx[t, 0:24] * pick(tab, ipx[t, 0:24]) * (u[t] - pltpu.roll(u[t], 1, 0)) for t in range(3)]
        gy = [fy[t, 0:24] * pick(tab, ipy[t, 0:24]) * (u[t] - down_y[t]) for t in range(3)]
        gz = [fz[t, 0:24] * pick(tab, ipz[t, 0:24]) * (u[t] - down_z[t]) for t in range(3)]
        up_y, up_z = shifted_up(gy, W), shifted_up(gz, 1)
        for t in range(3):
            total = (pltpu.roll(gx[t], PITCH - 1, 0) - gx[t]) + (up_y[t] - gy[t]) + (up_z[t] - gz[t])
            dl[t, s] = dl[t, s] - (fb[t, 0:24] * u[t] + total)
        return carry

    lax.fori_loop(0, S, coarse, 0)

    for t in range(3):
        hb[t, 16:24] = zero8
        for s in range(S):
            hb[t, s : s + 1] = dl[t, s, 0:1]
            hb[t, S + s : S + s + 1] = dl[t, s, W - 1 : W]

    def group_tiles(g):
        if g < 2 * S:
            return [dl[t, g // 2, 1 + 8 * (g % 2) : 9 + 8 * (g % 2)] for t in range(3)]
        return [hb[t, 8 * (g - 2 * S) : 8 * (g - 2 * S) + 8] for t in range(3)]

    main_from = ([0], [0, 1, 2], [1, 2, 3], [2, 3])
    rest_from = ([0, 1], [1, 2], [2, 3], [])
    for k in range(4):

        @pl.when(8 * k - y0 < W)
        def _(k=k):
            rest = None
            for g in range(GB):
                tiles = group_tiles(g) + [None]
                slot = 16 * (g % 8)

                def cut(number, amount, at):
                    value = zero8
                    for t in number:
                        piece = zero8 if tiles[t] is None else pltpu.roll(tiles[t], mod128(amount), 1)
                        value = jnp.where(lane >= 128 * t - at, piece, value)
                    return value

                back[owner + k, g] = cut(main_from[k], 512 - start[k], start[k])
                part = cut(rest_from[k], 512 - start[k] + slot, start[k] + 128 - slot)
                rest = part if slot == 0 else jnp.where(lane >= slot, part, rest)
                if slot == 112 or g == GB - 1:
                    back[owner + k, GB + g // 8] = rest


def add_windows(roots, arrived, acc, groups, stride):
    grp, me = lax.axis_index("grp"), lax.axis_index("dev")
    lane = lanes((8, 128))

    def clear(i, carry):
        acc[pl.ds(pl.multiple_of(8 * i, 8), 8), :] = jnp.zeros((8, 128), F32)
        return carry

    lax.fori_loop(0, stride, clear, 0)

    def one(p, carry):
        owner, y0, z0 = where_is(roots, grp * DEV + p)

        @pl.when(jnp.logical_and(me >= owner, 8 * (me - owner) - y0 < W))
        def _():
            window = jnp.logical_and(lane >= z0, lane < z0 + W)
            for number, g in enumerate(groups):
                main, rest = arrived[p, g], arrived[p, GB + g // 8]
                for y in range(8):
                    moved = pltpu.roll(main, mod128(z0 + 128 - W * y), 1)
                    if y == 7:
                        tail = pltpu.roll(rest, mod128(z0 + 2 + 128 - 16 * (g % 8)), 1)
                        moved = jnp.where(lane < z0 + 2, moved, tail)
                    rows = slice(y * stride + 8 * number, y * stride + 8 * number + 8)
                    acc[rows, :] = acc[rows, :] + jnp.where(window, moved, 0.0)

        return carry

    lax.fori_loop(0, DEV, one, 0)


def halo_kernel(roots, arrived, low, top, acc):
    add_windows(roots, arrived, acc, range(2 * S, GB), 24)
    for s in range(S):
        low[s] = acc[pl.ds(s, 8, stride=24), :]
        top[s] = acc[pl.ds(S + s, 8, stride=24), :]


def add_kernel(roots, arrived, coarse_one, out, acc):
    add_windows(roots, arrived, acc, range(2 * S), S * CX)
    for s in range(S):
        for x in range(CX):
            out[s, x] = coarse_one[s, x] + acc[pl.ds(s * CX + x, 8, stride=S * CX), :]


def call(kernel, outs, ins, scratch, name):
    return pl.pallas_call(
        kernel,
        out_shape=outs,
        in_specs=ins,
        out_specs=jax.tree.map(lambda _: VMEM, outs),
        scratch_shapes=scratch,
        compiler_params=pltpu.CompilerParams(vmem_limit_bytes=48 * 1024 * 1024),
        name=name,
    )


def shape(*dims):
    return jax.ShapeDtypeStruct(dims, F32)


def body(coarse_state, coef_index, coef_table, patch_root, fine_index):
    ends_g, ends_d = lax.axis_size("grp") - 1, lax.axis_size("dev") - 1
    up_g, down_g = [(i, i + 1) for i in range(ends_g)], [(i + 1, i) for i in range(ends_g)]
    up_d, down_d = [(i, i + 1) for i in range(ends_d)], [(i + 1, i) for i in range(ends_d)]
    known = jnp.concatenate([jnp.zeros((1, S), F32), coef_table], 0)
    pairs = (0.08 * (known[:, None] + known[None, :])).reshape(CLS * CLS, S)
    ptab = jnp.pad(pairs.T, ((0, 0), (0, 128 - CLS * CLS)))

    def plane(u, c):
        return jnp.concatenate([u, (c[None] + 1).astype(F32)], 0)

    x_lo = lax.ppermute(plane(coarse_state[:, CX - 1], coef_index[CX - 1]), "grp", up_g)
    x_hi = lax.ppermute(plane(coarse_state[:, 0], coef_index[0]), "grp", down_g)
    y_lo = lax.ppermute(plane(coarse_state[:, :, CY - 1], coef_index[:, CY - 1]), "dev", up_d)
    y_hi = lax.ppermute(plane(coarse_state[:, :, 0], coef_index[:, 0]), "dev", down_d)

    blocks = call(
        pack_kernel, shape(DEV, NF, 8, 128), [SMEM] + [VMEM] * 4, [pltpu.VMEM((8 * TR, 128), F32)], "pack"
    )(patch_root, coarse_state, coef_index, x_lo, x_hi)
    received = lax.all_to_all(blocks, "dev", split_axis=0, concat_axis=0, tiled=True)
    i32 = lambda *dims: pltpu.VMEM(dims, jnp.int32)
    f32 = lambda *dims: pltpu.VMEM(dims, F32)
    coarse_one = call(
        coarse_kernel,
        shape(S, CX, CY, 128),
        [VMEM] * 7,
        [i32(CX + 2, 8, 128), i32(CX + 1, 8, 128)] + [i32(CX, 8, 128)] * 4,
        "coarse",
    )(coarse_state, coef_index, x_lo, x_hi, y_lo, y_hi, ptab)

    tables = [jnp.asarray(w) for w in weights()]
    fine_state, corrections = call(
        patch_kernel,
        (shape(1, S, 32, 1024), shape(DEV, NB, 8, 128)),
        [SMEM] + [VMEM] * 7,
        [
            f32(3, CH, PITCH, 128), f32(24, CH, PITCH, 128), f32(CH, PITCH, 128),
            i32(8, 48, 128), i32(8, 40, 128), i32(9, 32, 128), i32(8, 32, 128), i32(8, 32, 128),
            f32(8, 48, 128), f32(8, 48, 128), f32(32, 128), f32(8, 32, 128),
            f32(8, 40, 128), f32(9, 32, 128), f32(8, 32, 128), f32(8, 32, 128),
            f32(8, 32, 128), f32(32, 128),
            f32(8, CH, PITCH, 128), f32(8, CH, PITCH, 128), f32(CH, PITCH, 128),
            f32(3, CH, PITCH, 128), f32(3, 24, 128),
        ],
        "patch",
    )(patch_root, received, fine_index, ptab, *tables)
    arrived = lax.all_to_all(corrections, "dev", split_axis=0, concat_axis=0, tiled=True)
    low, top = call(
        halo_kernel, (shape(S, CY, 128), shape(S, CY, 128)), [SMEM, VMEM], [f32(8 * 24, 128)], "halo"
    )(patch_root, arrived)
    from_above = lax.ppermute(low, "grp", down_g)
    from_below = lax.ppermute(top, "grp", up_g)
    coarse_new = call(
        add_kernel, shape(S, CX, CY, 128), [SMEM, VMEM, VMEM], [f32(8 * S * CX, 128)], "add"
    )(patch_root, arrived, coarse_one)
    coarse_new = coarse_new.at[:, CX - 1].add(from_above)
    coarse_new = coarse_new.at[:, 0].add(from_below)
    return coarse_new, fine_state


def solution(mesh):
    return jax.shard_map(
        body,
        mesh=mesh,
        in_specs=(
            P(None, "grp", "dev", None),
            P("grp", "dev", None),
            P(),
            P(),
            P(("grp", "dev"), None, None),
        ),
        out_specs=(P(None, "grp", "dev", None), P(("grp", "dev"), None, None, None)),
        check_vma=False,
    )
```

```python
import jax
import jax.numpy as jnp
import ml_dtypes
import numpy as np
from jax import lax
from jax.experimental import pallas as pl
from jax.experimental.pallas import tpu as pltpu
from jax.sharding import PartitionSpec as P

F32 = jnp.float32
S = 9
CH = 10
CX = 16
CY = 8
DEV = 16
W = 18
PITCH = 24
FRAME = W * W
BLK = CY * W
GF = 23
NF = GF + 3
GB = 21
NB = GB + 3
CLS = 9
VMEM = pl.BlockSpec(memory_space=pltpu.VMEM)
SMEM = pl.BlockSpec(memory_space=pltpu.SMEM)
ANY = pl.BlockSpec(memory_space=pl.ANY)


def weights():
    wf = np.zeros((128, 384), np.float32)
    rb = np.zeros((2, 128, 128), np.float32)
    for lane in range(128):
        q, fz = divmod(lane, 32)
        k, z = 1 + q // 2, fz // 2 + 1
        sy, sz = (0.125 if q % 2 else -0.125), (0.125 if fz % 2 else -0.125)
        wf[k * W + z, lane] += 1.0
        wf[(k + 1) * W + z, lane] += sy
        wf[(k - 1) * W + z, lane] -= sy
        wf[k * W + z + 1, lane] += sz
        wf[k * W + z - 1, lane] -= sz
        wf[k * W + z, 256 + lane] = 1.0
        rb[0, lane, (q // 2) * W + z] = 0.125
        if fz == 0:
            wf[k * W, 128 + lane] = 1.0
            rb[1, lane, (q // 2) * W] = 0.125
        if fz == 31:
            wf[k * W + W - 1, 128 + lane] = 1.0
            rb[1, lane, (q // 2) * W + W - 1] = 0.125
    wy = np.zeros((128, 128), np.float32)
    ry = np.zeros((128, 128), np.float32)
    for fz in range(32):
        z = fz // 2 + 1
        wy[z, 96 + fz] = 1.0
        wy[W + z, fz] = 1.0
        ry[fz, z] = 0.125
        ry[96 + fz, 50 + z] = 0.125
    wz = np.zeros((128, 256), np.float32)
    for lane in range(128):
        if lane % 32:
            wz[lane - 1, lane] = 1.0
        if lane % 32 != 31:
            wz[lane + 1, 128 + lane] = 1.0
    twice = lambda m: np.concatenate([m, m], 0).astype(ml_dtypes.bfloat16)
    return twice(np.concatenate([wf, wy, wz, ry, rb[0], rb[1]], 1))


def lanes(shape):
    return lax.broadcasted_iota(jnp.int32, shape, 1)


def mod128(x):
    return lax.bitwise_and(x, 127)


def halves(x):
    hi = x.astype(jnp.bfloat16)
    return hi, (x - hi.astype(F32)).astype(jnp.bfloat16)


def pick(tab, index):
    rows = index.shape[0]
    parts = [
        jnp.take_along_axis(tab, index[r : r + 8], axis=1, mode="promise_in_bounds") for r in range(0, rows, 8)
    ]
    return parts[0] if len(parts) == 1 else jnp.concatenate(parts, 0)


def where_is(roots, row):
    first = roots[row, 1] - 1
    owner = lax.shift_right_logical(first, 3)
    return owner, first - 8 * owner, roots[row, 2] - 1


def slab_kernel(u, idx, slab, ubuf, ibuf, sems):
    copies = [pltpu.make_async_copy(u.at[s], ubuf.at[s], sems.at[s]) for s in range(S)]
    copies.append(pltpu.make_async_copy(idx, ibuf, sems.at[S]))
    for copy in copies:
        copy.start()
    for s in range(S):
        copies[s].wait()
        for x in range(CX):
            slab[pl.ds(s * CX + x, 8, stride=CH * CX), :] = ubuf[s, x]
    copies[S].wait()
    for x in range(CX):
        slab[pl.ds(S * CX + x, 8, stride=CH * CX), :] = (ibuf[x] + 1).astype(F32)


def pack_kernel(roots, slab, lo, hi, out, halo):
    grp, me = lax.axis_index("grp"), lax.axis_index("dev")
    for c in range(CH):
        halo[pl.ds(c, 8, stride=24), :] = lo[c]
        halo[pl.ds(CH + c, 8, stride=24), :] = hi[c]
    for r in range(2 * CH, 24):
        halo[pl.ds(r, 8, stride=24), :] = jnp.zeros((8, 128), F32)
    lane = lanes((8, 128))

    def one(p, carry):
        owner, y0, z0 = where_is(roots, grp * DEV + p)

        @pl.when(jnp.logical_and(me >= owner, 8 * (me - owner) - y0 < W))
        def _():
            rest = None
            for g in range(GF):
                main = None
                for y in range(8):
                    if g < 2 * CH:
                        rows = slab[y * CH * CX + 8 * g : y * CH * CX + 8 * g + 8, :]
                    else:
                        rows = halo[y * 24 + 8 * (g - 2 * CH) : y * 24 + 8 * (g - 2 * CH) + 8, :]
                    moved = pltpu.roll(rows, mod128(W * y + 128 - z0), 1)
                    main = moved if y == 0 else jnp.where(lane >= W * y, moved, main)
                out[p, g] = main
                slot = 16 * (g % 8)
                moved = pltpu.roll(rows, mod128(126 + slot + 128 - z0), 1)
                rest = moved if slot == 0 else jnp.where(lane >= slot, moved, rest)
                if slot == 112 or g == GF - 1:
                    out[p, GF + g // 8] = rest

        return carry

    lax.fori_loop(0, DEV, one, 0)


def coarse_kernel(u, idx, lo, hi, ylo, yhi, ptab, _, out, cls, px, pyl, pyh, pzl, pzh):
    lane = lanes((8, 128))
    sub = lax.broadcasted_iota(jnp.int32, (8, 128), 0)
    cls[0] = lo[S].astype(jnp.int32)
    cls[CX + 1] = hi[S].astype(jnp.int32)
    for x in range(CX):
        cls[x + 1] = idx[x] + 1

    def below_y(a, row):
        return jnp.where(sub == 0, jnp.broadcast_to(row, (8, 128)), pltpu.roll(a, 1, 0))

    def above_y(a, row):
        return jnp.where(sub == 7, jnp.broadcast_to(row, (8, 128)), pltpu.roll(a, 7, 0))

    def below_z(a):
        return jnp.where(lane == 0, jnp.zeros_like(a), pltpu.roll(a, 1, 1))

    def above_z(a):
        return jnp.where(lane == 127, jnp.zeros_like(a), pltpu.roll(a, 127, 1))

    for x in range(CX + 1):
        px[x] = cls[x + 1] * CLS + cls[x]
    for x in range(CX):
        c = cls[x + 1]
        pyl[x] = c * CLS + below_y(c, ylo[S, x : x + 1, :].astype(jnp.int32))
        pyh[x] = c * CLS + above_y(c, yhi[S, x : x + 1, :].astype(jnp.int32))
        pzl[x] = c * CLS + below_z(c)
        pzh[x] = c * CLS + above_z(c)

    def species(s, carry):
        tab = jnp.broadcast_to(0.5 * ptab[pl.ds(s, 1), :], (8, 128))
        center = u[s, 0]
        flux = pick(tab, px[0]) * (center - lo[s])
        for x in range(CX):
            after = u[s, x + 1] if x + 1 < CX else hi[s]
            next_flux = pick(tab, px[x + 1]) * (after - center)
            total = next_flux - flux
            total = total + pick(tab, pyl[x]) * (below_y(center, ylo[s, x : x + 1, :]) - center)
            total = total + pick(tab, pyh[x]) * (above_y(center, yhi[s, x : x + 1, :]) - center)
            total = total + pick(tab, pzl[x]) * (below_z(center) - center)
            total = total + pick(tab, pzh[x]) * (above_z(center) - center)
            out[s, x] = center + total
            center, flux = after, next_flux
        return carry

    lax.fori_loop(0, S, species, 0)


def patch_kernel(
    roots, table, recv, fidx, tabs, _ylo, _yhi,
    fine, back,
    fr, fc, up, upy, da, ua, ub, uc, uy, dy, zg, dz, fx, fyl, fyh, fzl, fzh, fb, fs, gc, zr, yr, b1, b2, by, dl, mk, hb,
):
    grp, me = lax.axis_index("grp"), lax.axis_index("dev")
    owner, y0, _ = where_is(roots, grp * DEV + me)
    lane = lanes((8, 128))
    lane_all = lanes((2 * S * PITCH, 128))
    start = [BLK * k - W * y0 for k in range(4)]
    source = [jnp.minimum(owner + k, DEV - 1) for k in range(4)]
    zero8 = jnp.zeros((8, 128), F32)

    for t in range(3):
        for c in range(S):
            fr[t, c, 16:24] = zero8
        fc[t, 16:24] = zero8
    for g in range(GF):
        slot = 16 * (g % 8)
        main = [pltpu.roll(recv[source[k], g], mod128(start[k] + 256), 1) for k in range(4)]
        rest = [pltpu.roll(recv[source[k], GF + g // 8], mod128(start[k] + 384 - slot), 1) for k in range(3)]

        def over(t, piece, at, below):
            return jnp.where(lane >= at - 128 * t, piece, below)

        tile0 = over(0, main[1], start[1], over(0, rest[0], start[0] + 128, main[0]))
        tile1 = over(1, main[1], start[1], rest[0])
        tile1 = over(1, main[2], start[2], over(1, rest[1], start[1] + 128, tile1))
        tile2 = over(2, main[2], start[2], over(2, rest[1], start[1] + 128, main[1]))
        tile2 = over(2, main[3], start[3], over(2, rest[2], start[2] + 128, tile2))
        tile2 = jnp.where(lane < FRAME - 256, tile2, 0.0)
        for t, tile in enumerate((tile0, tile1, tile2)):
            if g < 2 * S:
                fr[t, g // 2, 1 + 8 * (g % 2) : 9 + 8 * (g % 2)] = tile
            elif g < 2 * CH:
                fc[t, 1 + 8 * (g % 2) : 9 + 8 * (g % 2)] = tile
            else:
                for i in range(8):
                    q = 8 * (g - 2 * CH) + i
                    if q < 2 * CH:
                        at = 0 if q < CH else W - 1
                        if q % CH < S:
                            fr[t, q % CH, at : at + 1] = tile[i : i + 1]
                        else:
                            fc[t, at : at + 1] = tile[i : i + 1]

    for t in range(3):
        for r in range(0, PITCH, 8):
            classes = fc[t, r : r + 8]
            masks = [classes == k + 1.0 for k in range(8)]
            for s in range(S):
                value = zero8
                for k in range(8):
                    value = jnp.where(masks[k], 0.08 * table[k, s], value)
                fr[t, S + s, r : r + 8] = value

    rows_all = 2 * S * PITCH

    def spread(values, weight):
        hi, lo = halves(values)
        return jnp.dot(jnp.concatenate([hi, lo], 1), weight, preferred_element_type=F32)

    for j in range(8):
        t, off = divmod(2 * W * j, 128)
        values = fr[t].reshape(rows_all, 128)
        if off:
            values = pltpu.roll(values, 128 - off, 1)
            if off + 4 * W > 128:
                after = pltpu.roll(fr[t + 1].reshape(rows_all, 128), 128 - off, 1)
                values = jnp.where(lane_all < 128 - off, values, after)
        result = spread(values, tabs[:, 0:384])
        for b in range(3):
            up[3 * j + b] = result[:, 128 * b : 128 * b + 128].reshape(2 * S, PITCH, 128)
    ends = jnp.where(
        lane_all < W,
        pltpu.roll(fr[2].reshape(rows_all, 128), 78, 1),
        pltpu.roll(fr[0].reshape(rows_all, 128), W, 1),
    )
    upy[...] = spread(ends, tabs[:, 384:512]).reshape(2 * S, PITCH, 128)

    for c in range(CH):
        for j in range(8):
            b1[j, c, 16:24] = zero8
            b2[j, c, 0:8] = zero8
            b2[j, c, 16:24] = zero8
            if c == S:
                b1[j, c, 0:8] = zero8
                b1[j, c, 8:16] = zero8
                b2[j, c, 8:16] = zero8
        by[c, 0:8] = zero8
        by[c, 16:24] = zero8
        if c == S:
            by[c, 8:16] = zero8
    for j in range(8):
        da[j, 40:48] = zero8

    lane32 = lanes((32, 128))
    z_low = lax.bitwise_and(lane32, 31) == 0
    z_top = lax.bitwise_and(lane32, 31) == 31
    inner = slice(8, 40)

    def twice(ref, at, values):
        ref[at + (pl.ds(0, CX, stride=2), slice(None))] = values
        ref[at + (pl.ds(1, CX, stride=2), slice(None))] = values

    def z_neighbours(tiles):
        result = spread(jnp.concatenate(tiles, 0), tabs[:, 512:768])
        return [(result[32 * j : 32 * j + 32, :128], result[32 * j : 32 * j + 32, 128:]) for j in range(8)]

    def y_neighbours(tiles, ghost):
        down = [pltpu.roll(a, 32, 1) for a in tiles]
        above = [pltpu.roll(a, 96, 1) for a in tiles]
        low = [jnp.where(lane32 < 32, down[j - 1] if j else ghost, down[j]) for j in range(8)]
        top = [jnp.where(lane32 < 96, above[j], above[j + 1] if j < 7 else ghost) for j in range(8)]
        return low, top

    def change(j, src, u, low, top, z):
        value = fx[j, 0:32] * src[j, 7:39] + fx[j, 1:33] * src[j, 9:41]
        value = value + (fyl[j] * low[j] + fyh[j] * top[j])
        value = value + (fzl[j] * z[j][0] + fzh[j] * z[j][1])
        return u + (value + (gc[j] - fs[j] * u))

    def species(s, carry):
        for j in range(8):
            core, dcore = up[3 * j + 2, s], up[3 * j + 2, S + s]
            slope = 0.125 * (up[3 * j + 2, s, 2 : CX + 2] - up[3 * j + 2, s, 0:CX])
            middle = up[3 * j, s, 1 : CX + 1]
            ua[j, pl.ds(8, CX, stride=2), :] = middle - slope
            ua[j, pl.ds(9, CX, stride=2), :] = middle + slope
            for ref, values in ((ua, core), (ub, core), (da, dcore)):
                ref[j, 7:8] = values[0:1]
                ref[j, 40:41] = values[W - 1 : W]
            twice(zg, (j,), up[3 * j + 1, s, 1 : CX + 1])
            twice(dz, (j,), up[3 * j + 1, S + s, 1 : CX + 1])
        twice(uy, (), upy[s, 1 : CX + 1])
        twice(dy, (), upy[S + s, 1 : CX + 1])

        known = [0.08 * table[k, s] for k in range(8)]
        diffs = []
        for j in range(8):
            index = fidx[0, :, 128 * j : 128 * j + 128]
            one, two, four = [lax.bitwise_and(index, bit) != 0 for bit in (1, 2, 4)]
            level = [jnp.where(one, known[k + 1], known[k]) for k in (0, 2, 4, 6)]
            level = [jnp.where(two, level[1], level[0]), jnp.where(two, level[3], level[2])]
            diffs.append(jnp.where(four, level[1], level[0]))
            da[j, inner] = diffs[j]
        z = z_neighbours(diffs)
        low, top = y_neighbours(diffs, dy[...])
        for j in range(8):
            d = diffs[j]
            fx[j] = da[j, 8:48] + da[j, 7:47]
            fyl[j] = d + low[j]
            fyh[j] = d + top[j]
            ghost = dz[j]
            low_z = d + jnp.where(z_low, ghost, z[j][0])
            top_z = d + jnp.where(z_top, ghost, z[j][1])
            fzl[j] = low_z
            fzh[j] = top_z
            edge = jnp.where(z_low, low_z, jnp.where(z_top, top_z, 0.0))
            fb[j] = edge
            gc[j] = edge * zg[j]
            fs[j] = ((fx[j, 0:32] + fx[j, 1:33]) + (fyl[j] + fyh[j])) + (low_z + top_z)

        first = [ua[j, inner] for j in range(8)]
        z = z_neighbours(first)
        ghost = uy[...]
        low, top = y_neighbours(first, ghost)
        for j in range(8):
            ub[j, inner] = change(j, ua, first[j], low, top, z)
        second = [ub[j, inner] for j in range(8)]
        z = z_neighbours(second)
        low, top = y_neighbours(second, ghost)
        for j in range(8):
            both = ua[j, inner] + second[j]
            value = change(j, ub, second[j], low, top, z)
            uc[j] = value
            fine[0, s, :, 128 * j : 128 * j + 128] = value
            zr[j] = fb[j] * both - 2.0 * gc[j]
            for at, row, out_row in ((0, 8, 0), (32, 39, W - 1)):
                outer = 7 if row == 8 else 40
                total = ua[j, row : row + 1] + ub[j, row : row + 1] - 2.0 * ua[j, outer : outer + 1]
                b1[j, s, out_row : out_row + 1] = fx[j, at : at + 1] * total
            if j == 0:
                yr[...] = jnp.where(lane32 < 32, fyl[0] * (both - 2.0 * ghost), 0.0)
            if j == 7:
                yr[...] = jnp.where(lane32 < 96, yr[...], fyh[7] * (both - 2.0 * ghost))
        for j in range(8):
            b1[j, s, 1 : CX + 1] = uc[j, pl.ds(0, CX, stride=2), :] + uc[j, pl.ds(1, CX, stride=2), :]
            b2[j, s, 1 : CX + 1] = zr[j, pl.ds(0, CX, stride=2), :] + zr[j, pl.ds(1, CX, stride=2), :]
        by[s, 1 : CX + 1] = yr[pl.ds(0, CX, stride=2), :] + yr[pl.ds(1, CX, stride=2), :]
        return carry

    lax.fori_loop(0, S, species, 0)

    lane_out = lanes((CH * PITCH, 128))
    delta = [jnp.zeros((CH * PITCH, 128), F32) for _ in range(3)]
    for j in range(8):
        t, off = divmod(2 * W * j + W, 128)
        sums = spread(b1[j].reshape(CH * PITCH, 128), tabs[:, 896:1024])
        sums = pltpu.roll(sums + spread(b2[j].reshape(CH * PITCH, 128), tabs[:, 1024:1152]), off, 1)
        if off + 2 * W > 128:
            delta[t] = delta[t] + jnp.where(lane_out >= off, sums, 0.0)
            delta[t + 1] = delta[t + 1] + jnp.where(lane_out < off, sums, 0.0)
        else:
            delta[t] = delta[t] + sums
    sums = spread(by[...].reshape(CH * PITCH, 128), tabs[:, 768:896])
    delta[0] = delta[0] + jnp.where(lane_out < W, sums, 0.0)
    delta[2] = delta[2] + jnp.where(lane_out >= 50, sums, 0.0)
    for t in range(3):
        dl[t] = delta[t].reshape(CH, PITCH, 128)

    rows3 = 3 * PITCH
    lane_c = lanes((rows3, 128))
    lane24 = lanes((PITCH, 128))
    row24 = lax.broadcasted_iota(jnp.int32, (PITCH, 128), 0)

    def within(a, top):
        return jnp.logical_and(a >= 1, a <= top)

    def shifted_down(tiles, by_lanes):
        moved = [pltpu.roll(a, by_lanes, 1) for a in tiles]
        return [jnp.where(lane_c < by_lanes, moved[t - 1], moved[t]) for t in range(3)]

    def shifted_up(tiles, by_lanes):
        moved = [pltpu.roll(a, 128 - by_lanes, 1) for a in tiles]
        return [jnp.where(lane_c < 128 - by_lanes, moved[t], moved[(t + 1) % 3]) for t in range(3)]

    for t in range(3):
        cell = lane24 + 128 * t
        y = lax.shift_right_logical(cell * 3641, 16)
        z = cell - W * y
        inside = [within(row24, CX), within(y, CX), within(z, CX)]
        wider = [within(row24, CX + 1), within(y, CX + 1), within(z, CX + 1)]
        every = lambda a, b, c: jnp.logical_and(a, jnp.logical_and(b, c))
        faces = [every(*(wider[n] if n == axis else inside[n] for n in range(3))) for axis in range(3)]
        for i in range(3):
            for axis in range(3):
                mk[3 * axis + t, 24 * i : 24 * i + 24] = jnp.where(faces[axis], 0.5, 0.0)
            mk[9 + t, 24 * i : 24 * i + 24] = jnp.where(every(*inside), 1.0, 0.0)

    def coarse(i, carry):
        u = [fr[t, pl.ds(3 * i, 3)].reshape(rows3, 128) for t in range(3)]
        d = [fr[t, pl.ds(S + 3 * i, 3)].reshape(rows3, 128) for t in range(3)]
        below = [[pltpu.roll(a, 1, 0) for a in v] for v in (u, d)]
        flux = [[mk[t] * (d[t] + below[1][t]) * (u[t] - below[0][t]) for t in range(3)]]
        for axis, step in ((1, W), (2, 1)):
            down = [shifted_down(v, step) for v in (u, d)]
            flux.append([mk[3 * axis + t] * (d[t] + down[1][t]) * (u[t] - down[0][t]) for t in range(3)])
        up_y, up_z = shifted_up(flux[1], W), shifted_up(flux[2], 1)
        for t in range(3):
            total = pltpu.roll(flux[0][t], rows3 - 1, 0) - flux[0][t]
            total = total + (up_y[t] - flux[1][t]) + (up_z[t] - flux[2][t])
            old = dl[t, pl.ds(3 * i, 3)].reshape(rows3, 128)
            dl[t, pl.ds(3 * i, 3)] = (old - (mk[9 + t] * u[t] + total)).reshape(3, PITCH, 128)
        return carry

    lax.fori_loop(0, S // 3, coarse, 0)

    for t in range(3):
        hb[t, 16:24] = zero8
        for s in range(S):
            hb[t, s : s + 1] = dl[t, s, 0:1]
            hb[t, S + s : S + s + 1] = dl[t, s, W - 1 : W]

    def group_tiles(g):
        if g < 2 * S:
            return [dl[t, g // 2, 1 + 8 * (g % 2) : 9 + 8 * (g % 2)] for t in range(3)]
        return [hb[t, 8 * (g - 2 * S) : 8 * (g - 2 * S) + 8] for t in range(3)]

    main_from = ([0], [0, 1, 2], [1, 2, 3], [2, 3])
    rest_from = ([0, 1], [1, 2], [2, 3], [])
    for k in range(4):

        @pl.when(8 * k - y0 < W)
        def _(k=k):
            rest = None
            for g in range(GB):
                tiles = group_tiles(g) + [None]
                slot = 16 * (g % 8)

                def cut(number, amount, at):
                    value = zero8
                    for t in number:
                        piece = zero8 if tiles[t] is None else pltpu.roll(tiles[t], mod128(amount), 1)
                        value = jnp.where(lane >= 128 * t - at, piece, value)
                    return value

                back[owner + k, g] = cut(main_from[k], 512 - start[k], start[k])
                part = cut(rest_from[k], 512 - start[k] + slot, start[k] + 128 - slot)
                rest = part if slot == 0 else jnp.where(lane >= slot, part, rest)
                if slot == 112 or g == GB - 1:
                    back[owner + k, GB + g // 8] = rest


def add_windows(roots, arrived, acc, groups, stride):
    grp, me = lax.axis_index("grp"), lax.axis_index("dev")
    lane = lanes((8, 128))

    def clear(i, carry):
        acc[pl.ds(pl.multiple_of(8 * i, 8), 8), :] = jnp.zeros((8, 128), F32)
        return carry

    lax.fori_loop(0, stride, clear, 0)

    def one(p, carry):
        owner, y0, z0 = where_is(roots, grp * DEV + p)

        @pl.when(jnp.logical_and(me >= owner, 8 * (me - owner) - y0 < W))
        def _():
            window = jnp.logical_and(lane >= z0, lane < z0 + W)
            for number, g in enumerate(groups):
                main, rest = arrived[p, g], arrived[p, GB + g // 8]
                for y in range(8):
                    moved = pltpu.roll(main, mod128(z0 + 128 - W * y), 1)
                    if y == 7:
                        tail = pltpu.roll(rest, mod128(z0 + 2 + 128 - 16 * (g % 8)), 1)
                        moved = jnp.where(lane < z0 + 2, moved, tail)
                    rows = slice(y * stride + 8 * number, y * stride + 8 * number + 8)
                    acc[rows, :] = acc[rows, :] + jnp.where(window, moved, 0.0)

        return carry

    lax.fori_loop(0, DEV, one, 0)


def halo_kernel(roots, arrived, _, low, top, acc):
    add_windows(roots, arrived, acc, range(2 * S, GB), 24)
    for s in range(S):
        low[s] = acc[pl.ds(s, 8, stride=24), :]
        top[s] = acc[pl.ds(S + s, 8, stride=24), :]


def add_kernel(roots, arrived, coarse_one, below, above, out, acc):
    add_windows(roots, arrived, acc, range(2 * S), S * CX)
    for s in range(S):
        for x in range(CX):
            value = coarse_one[s, x] + acc[pl.ds(s * CX + x, 8, stride=S * CX), :]
            if x == 0:
                value = value + below[s]
            if x == CX - 1:
                value = value + above[s]
            out[s, x] = value


def call(kernel, outs, ins, scratch, name, mib):
    return pl.pallas_call(
        kernel,
        out_shape=outs,
        in_specs=ins,
        out_specs=jax.tree.map(lambda _: VMEM, outs),
        scratch_shapes=scratch,
        compiler_params=pltpu.CompilerParams(vmem_limit_bytes=mib * 1024 * 1024),
        name=name,
    )


def shape(*dims):
    return jax.ShapeDtypeStruct(dims, F32)


def body(coarse_state, coef_index, coef_table, patch_root, fine_index):
    ends_g, ends_d = lax.axis_size("grp") - 1, lax.axis_size("dev") - 1
    up_g, down_g = [(i, i + 1) for i in range(ends_g)], [(i + 1, i) for i in range(ends_g)]
    up_d, down_d = [(i, i + 1) for i in range(ends_d)], [(i + 1, i) for i in range(ends_d)]
    known = jnp.concatenate([jnp.zeros((1, S), F32), coef_table], 0)
    pairs = (0.08 * (known[:, None] + known[None, :])).reshape(CLS * CLS, S)
    ptab = jnp.pad(pairs.T, ((0, 0), (0, 128 - CLS * CLS)))

    def plane(u, c):
        return jnp.concatenate([u, (c[None] + 1).astype(F32)], 0)

    x_lo = lax.ppermute(plane(coarse_state[:, CX - 1], coef_index[CX - 1]), "grp", up_g)
    x_hi = lax.ppermute(plane(coarse_state[:, 0], coef_index[0]), "grp", down_g)
    y_lo = lax.ppermute(plane(coarse_state[:, :, CY - 1], coef_index[:, CY - 1]), "dev", up_d)
    y_hi = lax.ppermute(plane(coarse_state[:, :, 0], coef_index[:, 0]), "dev", down_d)

    slab = call(
        slab_kernel,
        shape(CY * CH * CX, 128),
        [ANY] * 2,
        [
            pltpu.VMEM((S, CX, CY, 128), F32),
            pltpu.VMEM((CX, CY, 128), jnp.int32),
            pltpu.SemaphoreType.DMA((CH,)),
        ],
        "slab",
        8,
    )(coarse_state, coef_index)
    blocks = call(
        pack_kernel, shape(DEV, NF, 8, 128), [SMEM] + [VMEM] * 3, [pltpu.VMEM((8 * 24, 128), F32)], "pack", 8
    )(patch_root, slab, x_lo, x_hi)
    received = lax.all_to_all(blocks, "dev", split_axis=0, concat_axis=0, tiled=True)
    i32 = lambda *dims: pltpu.VMEM(dims, jnp.int32)
    f32 = lambda *dims: pltpu.VMEM(dims, F32)
    fine_state, corrections = call(
        patch_kernel,
        (shape(1, S, 32, 1024), shape(DEV, NB, 8, 128)),
        [SMEM, SMEM] + [VMEM] * 3 + [ANY] * 2,
        [
            f32(3, 2 * S, PITCH, 128), f32(3, PITCH, 128), f32(24, 2 * S, PITCH, 128), f32(2 * S, PITCH, 128),
            f32(8, 48, 128), f32(8, 48, 128), f32(8, 48, 128), f32(8, 32, 128),
            f32(32, 128), f32(32, 128), f32(8, 32, 128), f32(8, 32, 128),
            f32(8, 40, 128), f32(8, 32, 128), f32(8, 32, 128), f32(8, 32, 128), f32(8, 32, 128),
            f32(8, 32, 128), f32(8, 32, 128), f32(8, 32, 128), f32(8, 32, 128), f32(32, 128),
            f32(8, CH, PITCH, 128), f32(8, CH, PITCH, 128), f32(CH, PITCH, 128),
            f32(3, CH, PITCH, 128), f32(12, 3 * PITCH, 128), f32(3, 24, 128),
        ],
        "patch",
        32,
    )(patch_root, coef_table, received, fine_index, jnp.asarray(weights()), y_lo, y_hi)
    arrived = lax.all_to_all(corrections, "dev", split_axis=0, concat_axis=0, tiled=True)
    coarse_one = call(
        coarse_kernel,
        shape(S, CX, CY, 128),
        [VMEM] * 7 + [ANY],
        [i32(CX + 2, 8, 128), i32(CX + 1, 8, 128)] + [i32(CX, 8, 128)] * 4,
        "coarse",
        8,
    )(coarse_state, coef_index, x_lo, x_hi, y_lo, y_hi, ptab, corrections)
    low, top = call(
        halo_kernel, (shape(S, CY, 128), shape(S, CY, 128)), [SMEM, VMEM, ANY], [f32(8 * 24, 128)], "halo", 8
    )(patch_root, arrived, coarse_one)
    from_above = lax.ppermute(low, "grp", down_g)
    from_below = lax.ppermute(top, "grp", up_g)
    coarse_new = call(
        add_kernel, shape(S, CX, CY, 128), [SMEM] + [VMEM] * 4, [f32(8 * S * CX, 128)], "add", 8
    )(patch_root, arrived, coarse_one, from_below, from_above)
    return coarse_new, fine_state


def solution(mesh):
    return jax.shard_map(
        body,
        mesh=mesh,
        in_specs=(
            P(None, "grp", "dev", None),
            P("grp", "dev", None),
            P(),
            P(),
            P(("grp", "dev"), None, None),
        ),
        out_specs=(P(None, "grp", "dev", None), P(("grp", "dev"), None, None, None)),
        check_vma=False,
    )
```

```python
import jax
import jax.numpy as jnp
import ml_dtypes
import numpy as np
from jax import lax
from jax.experimental import pallas as pl
from jax.experimental.pallas import tpu as pltpu
from jax.sharding import PartitionSpec as P

F32 = jnp.float32
S = 9
CH = 10
CX = 16
CY = 8
DEV = 16
W = 18
PITCH = 24
FRAME = W * W
BLK = CY * W
GF = 23
NF = GF + 3
GB = 21
NB = GB + 3
CLS = 9
VMEM = pl.BlockSpec(memory_space=pltpu.VMEM)
SMEM = pl.BlockSpec(memory_space=pltpu.SMEM)
ANY = pl.BlockSpec(memory_space=pl.ANY)


def weights():
    wf = np.zeros((128, 384), np.float32)
    rb = np.zeros((2, 128, 128), np.float32)
    for lane in range(128):
        q, fz = divmod(lane, 32)
        k, z = 1 + q // 2, fz // 2 + 1
        sy, sz = (0.125 if q % 2 else -0.125), (0.125 if fz % 2 else -0.125)
        wf[k * W + z, lane] += 1.0
        wf[(k + 1) * W + z, lane] += sy
        wf[(k - 1) * W + z, lane] -= sy
        wf[k * W + z + 1, lane] += sz
        wf[k * W + z - 1, lane] -= sz
        wf[k * W + z, 256 + lane] = 1.0
        rb[0, lane, (q // 2) * W + z] = 0.125
        if fz == 0:
            wf[k * W, 128 + lane] = 1.0
            rb[1, lane, (q // 2) * W] = 0.125
        if fz == 31:
            wf[k * W + W - 1, 128 + lane] = 1.0
            rb[1, lane, (q // 2) * W + W - 1] = 0.125
    wy = np.zeros((128, 128), np.float32)
    ry = np.zeros((128, 128), np.float32)
    for fz in range(32):
        z = fz // 2 + 1
        wy[z, 96 + fz] = 1.0
        wy[W + z, fz] = 1.0
        ry[fz, z] = 0.125
        ry[96 + fz, 50 + z] = 0.125
    wz = np.zeros((128, 256), np.float32)
    for lane in range(128):
        if lane % 32:
            wz[lane - 1, lane] = 1.0
        if lane % 32 != 31:
            wz[lane + 1, 128 + lane] = 1.0
    twice = lambda m: np.concatenate([m, m], 0).astype(ml_dtypes.bfloat16)
    return twice(np.concatenate([wf, wy, wz, ry, rb[0], rb[1]], 1))


def lanes(shape):
    return lax.broadcasted_iota(jnp.int32, shape, 1)


def mod128(x):
    return lax.bitwise_and(x, 127)


def halves(x):
    hi = x.astype(jnp.bfloat16)
    return hi, (x - hi.astype(F32)).astype(jnp.bfloat16)


def pick(tab, index):
    rows = index.shape[0]
    parts = [
        jnp.take_along_axis(tab, index[r : r + 8], axis=1, mode="promise_in_bounds") for r in range(0, rows, 8)
    ]
    return parts[0] if len(parts) == 1 else jnp.concatenate(parts, 0)


def where_is(roots, row):
    first = roots[row, 1] - 1
    owner = lax.shift_right_logical(first, 3)
    return owner, first - 8 * owner, roots[row, 2] - 1


def slab_kernel(u, idx, slab, ubuf, ibuf, sems):
    copies = [pltpu.make_async_copy(u.at[s], ubuf.at[s], sems.at[s]) for s in range(S)]
    copies.append(pltpu.make_async_copy(idx, ibuf, sems.at[S]))
    for copy in copies:
        copy.start()
    for s in range(S):
        copies[s].wait()
        for x in range(CX):
            slab[pl.ds(s * CX + x, 8, stride=CH * CX), :] = ubuf[s, x]
    copies[S].wait()
    for x in range(CX):
        slab[pl.ds(S * CX + x, 8, stride=CH * CX), :] = (ibuf[x] + 1).astype(F32)


def pack_kernel(roots, slab, lo, hi, out, halo):
    grp, me = lax.axis_index("grp"), lax.axis_index("dev")
    for c in range(CH):
        halo[pl.ds(c, 8, stride=24), :] = lo[c]
        halo[pl.ds(CH + c, 8, stride=24), :] = hi[c]
    for r in range(2 * CH, 24):
        halo[pl.ds(r, 8, stride=24), :] = jnp.zeros((8, 128), F32)
    lane = lanes((8, 128))

    def one(p, carry):
        owner, y0, z0 = where_is(roots, grp * DEV + p)

        @pl.when(jnp.logical_and(me >= owner, 8 * (me - owner) - y0 < W))
        def _():
            rest = None
            for g in range(GF):
                main = None
                for y in range(8):
                    if g < 2 * CH:
                        rows = slab[y * CH * CX + 8 * g : y * CH * CX + 8 * g + 8, :]
                    else:
                        rows = halo[y * 24 + 8 * (g - 2 * CH) : y * 24 + 8 * (g - 2 * CH) + 8, :]
                    moved = pltpu.roll(rows, mod128(W * y + 128 - z0), 1)
                    main = moved if y == 0 else jnp.where(lane >= W * y, moved, main)
                out[p, g] = main
                slot = 16 * (g % 8)
                moved = pltpu.roll(rows, mod128(126 + slot + 128 - z0), 1)
                rest = moved if slot == 0 else jnp.where(lane >= slot, moved, rest)
                if slot == 112 or g == GF - 1:
                    out[p, GF + g // 8] = rest

        return carry

    lax.fori_loop(0, DEV, one, 0)


def coarse_kernel(u, idx, lo, hi, ptab, _, out, cls, px, pyl, pyh, pzl, pzh):
    lane = lanes((8, 128))
    sub = lax.broadcasted_iota(jnp.int32, (8, 128), 0)
    cls[0] = lo[S].astype(jnp.int32)
    cls[CX + 1] = hi[S].astype(jnp.int32)
    for x in range(CX):
        cls[x + 1] = idx[x] + 1

    def below_z(a):
        return jnp.where(lane == 0, jnp.zeros_like(a), pltpu.roll(a, 1, 1))

    def above_z(a):
        return jnp.where(lane == 127, jnp.zeros_like(a), pltpu.roll(a, 127, 1))

    for x in range(CX + 1):
        px[x] = cls[x + 1] * CLS + cls[x]
    for x in range(CX):
        c = cls[x + 1]
        pyl[x] = jnp.where(sub == 0, 127, c * CLS + pltpu.roll(c, 1, 0))
        pyh[x] = jnp.where(sub == 7, 127, c * CLS + pltpu.roll(c, 7, 0))
        pzl[x] = c * CLS + below_z(c)
        pzh[x] = c * CLS + above_z(c)

    def species(s, carry):
        tab = jnp.broadcast_to(0.5 * ptab[pl.ds(s, 1), :], (8, 128))
        center = u[s, 0]
        flux = pick(tab, px[0]) * (center - lo[s])
        for x in range(CX):
            after = u[s, x + 1] if x + 1 < CX else hi[s]
            next_flux = pick(tab, px[x + 1]) * (after - center)
            total = next_flux - flux
            total = total + pick(tab, pyl[x]) * (pltpu.roll(center, 1, 0) - center)
            total = total + pick(tab, pyh[x]) * (pltpu.roll(center, 7, 0) - center)
            total = total + pick(tab, pzl[x]) * (below_z(center) - center)
            total = total + pick(tab, pzh[x]) * (above_z(center) - center)
            out[s, x] = center + total
            center, flux = after, next_flux
        return carry

    lax.fori_loop(0, S, species, 0)


def patch_kernel(
    roots, table, recv, fidx, tabs,
    fine, back,
    fr, fc, up, upy, da, ua, ub, uc, uy, dy, zg, dz, fx, fyl, fyh, fzl, fzh, fb, fs, gc, zr, yr, b1, b2, by, dl, mk, hb, fbuf, bbuf, fsem, bsem,
):
    grp, me = lax.axis_index("grp"), lax.axis_index("dev")
    owner, y0, _ = where_is(roots, grp * DEV + me)
    lane = lanes((8, 128))
    lane_all = lanes((2 * S * PITCH, 128))
    start = [BLK * k - W * y0 for k in range(4)]
    source = [jnp.minimum(owner + k, DEV - 1) for k in range(4)]
    zero8 = jnp.zeros((8, 128), F32)

    for t in range(3):
        for c in range(S):
            fr[t, c, 16:24] = zero8
        fc[t, 16:24] = zero8
    for g in range(GF):
        slot = 16 * (g % 8)
        main = [pltpu.roll(recv[source[k], g], mod128(start[k] + 256), 1) for k in range(4)]
        rest = [pltpu.roll(recv[source[k], GF + g // 8], mod128(start[k] + 384 - slot), 1) for k in range(3)]

        def over(t, piece, at, below):
            return jnp.where(lane >= at - 128 * t, piece, below)

        tile0 = over(0, main[1], start[1], over(0, rest[0], start[0] + 128, main[0]))
        tile1 = over(1, main[1], start[1], rest[0])
        tile1 = over(1, main[2], start[2], over(1, rest[1], start[1] + 128, tile1))
        tile2 = over(2, main[2], start[2], over(2, rest[1], start[1] + 128, main[1]))
        tile2 = over(2, main[3], start[3], over(2, rest[2], start[2] + 128, tile2))
        tile2 = jnp.where(lane < FRAME - 256, tile2, 0.0)
        for t, tile in enumerate((tile0, tile1, tile2)):
            if g < 2 * S:
                fr[t, g // 2, 1 + 8 * (g % 2) : 9 + 8 * (g % 2)] = tile
            elif g < 2 * CH:
                fc[t, 1 + 8 * (g % 2) : 9 + 8 * (g % 2)] = tile
            else:
                for i in range(8):
                    q = 8 * (g - 2 * CH) + i
                    if q < 2 * CH:
                        at = 0 if q < CH else W - 1
                        if q % CH < S:
                            fr[t, q % CH, at : at + 1] = tile[i : i + 1]
                        else:
                            fc[t, at : at + 1] = tile[i : i + 1]

    for t in range(3):
        for r in range(0, PITCH, 8):
            classes = fc[t, r : r + 8]
            masks = [classes == k + 1.0 for k in range(8)]
            for s in range(S):
                value = zero8
                for k in range(8):
                    value = jnp.where(masks[k], 0.08 * table[k, s], value)
                fr[t, S + s, r : r + 8] = value

    rows_all = 2 * S * PITCH

    def spread(values, weight):
        hi, lo = halves(values)
        return jnp.dot(jnp.concatenate([hi, lo], 1), weight, preferred_element_type=F32)

    for j in range(8):
        t, off = divmod(2 * W * j, 128)
        values = fr[t].reshape(rows_all, 128)
        if off:
            values = pltpu.roll(values, 128 - off, 1)
            if off + 4 * W > 128:
                after = pltpu.roll(fr[t + 1].reshape(rows_all, 128), 128 - off, 1)
                values = jnp.where(lane_all < 128 - off, values, after)
        result = spread(values, tabs[:, 0:384])
        for b in range(3):
            up[3 * j + b] = result[:, 128 * b : 128 * b + 128].reshape(2 * S, PITCH, 128)
    ends = jnp.where(
        lane_all < W,
        pltpu.roll(fr[2].reshape(rows_all, 128), 78, 1),
        pltpu.roll(fr[0].reshape(rows_all, 128), W, 1),
    )
    upy[...] = spread(ends, tabs[:, 384:512]).reshape(2 * S, PITCH, 128)

    for c in range(CH):
        for j in range(8):
            b1[j, c, 16:24] = zero8
            b2[j, c, 0:8] = zero8
            b2[j, c, 16:24] = zero8
            if c == S:
                b1[j, c, 0:8] = zero8
                b1[j, c, 8:16] = zero8
                b2[j, c, 8:16] = zero8
        by[c, 0:8] = zero8
        by[c, 16:24] = zero8
        if c == S:
            by[c, 8:16] = zero8
    for j in range(8):
        da[j, 40:48] = zero8

    lane32 = lanes((32, 128))
    z_low = lax.bitwise_and(lane32, 31) == 0
    z_top = lax.bitwise_and(lane32, 31) == 31
    inner = slice(8, 40)

    def twice(ref, at, values):
        ref[at + (pl.ds(0, CX, stride=2), slice(None))] = values
        ref[at + (pl.ds(1, CX, stride=2), slice(None))] = values

    def z_neighbours(tiles):
        result = spread(jnp.concatenate(tiles, 0), tabs[:, 512:768])
        return [(result[32 * j : 32 * j + 32, :128], result[32 * j : 32 * j + 32, 128:]) for j in range(8)]

    def y_neighbours(tiles, ghost):
        down = [pltpu.roll(a, 32, 1) for a in tiles]
        above = [pltpu.roll(a, 96, 1) for a in tiles]
        low = [jnp.where(lane32 < 32, down[j - 1] if j else ghost, down[j]) for j in range(8)]
        top = [jnp.where(lane32 < 96, above[j], above[j + 1] if j < 7 else ghost) for j in range(8)]
        return low, top

    def change(j, src, u, low, top, z):
        value = fx[j, 0:32] * src[j, 7:39] + fx[j, 1:33] * src[j, 9:41]
        value = value + (fyl[j] * low[j] + fyh[j] * top[j])
        value = value + (fzl[j] * z[j][0] + fzh[j] * z[j][1])
        return u + (value + (gc[j] - fs[j] * u))

    def leave(s):
        half = lax.bitwise_and(s, 1)
        return pltpu.make_async_copy(fbuf.at[half], fine.at[0, s], fsem.at[half])

    def species(s, carry):
        for j in range(8):
            core, dcore = up[3 * j + 2, s], up[3 * j + 2, S + s]
            slope = 0.125 * (up[3 * j + 2, s, 2 : CX + 2] - up[3 * j + 2, s, 0:CX])
            middle = up[3 * j, s, 1 : CX + 1]
            ua[j, pl.ds(8, CX, stride=2), :] = middle - slope
            ua[j, pl.ds(9, CX, stride=2), :] = middle + slope
            for ref, values in ((ua, core), (ub, core), (da, dcore)):
                ref[j, 7:8] = values[0:1]
                ref[j, 40:41] = values[W - 1 : W]
            twice(zg, (j,), up[3 * j + 1, s, 1 : CX + 1])
            twice(dz, (j,), up[3 * j + 1, S + s, 1 : CX + 1])
        twice(uy, (), upy[s, 1 : CX + 1])
        twice(dy, (), upy[S + s, 1 : CX + 1])

        known = [0.08 * table[k, s] for k in range(8)]
        diffs = []
        for j in range(8):
            index = fidx[0, :, 128 * j : 128 * j + 128]
            one, two, four = [lax.bitwise_and(index, bit) != 0 for bit in (1, 2, 4)]
            level = [jnp.where(one, known[k + 1], known[k]) for k in (0, 2, 4, 6)]
            level = [jnp.where(two, level[1], level[0]), jnp.where(two, level[3], level[2])]
            diffs.append(jnp.where(four, level[1], level[0]))
            da[j, inner] = diffs[j]
        z = z_neighbours(diffs)
        low, top = y_neighbours(diffs, dy[...])
        for j in range(8):
            d = diffs[j]
            fx[j] = da[j, 8:48] + da[j, 7:47]
            fyl[j] = d + low[j]
            fyh[j] = d + top[j]
            ghost = dz[j]
            low_z = d + jnp.where(z_low, ghost, z[j][0])
            top_z = d + jnp.where(z_top, ghost, z[j][1])
            fzl[j] = low_z
            fzh[j] = top_z
            edge = jnp.where(z_low, low_z, jnp.where(z_top, top_z, 0.0))
            fb[j] = edge
            gc[j] = edge * zg[j]
            fs[j] = ((fx[j, 0:32] + fx[j, 1:33]) + (fyl[j] + fyh[j])) + (low_z + top_z)

        first = [ua[j, inner] for j in range(8)]
        z = z_neighbours(first)
        ghost = uy[...]
        low, top = y_neighbours(first, ghost)
        for j in range(8):
            ub[j, inner] = change(j, ua, first[j], low, top, z)
        second = [ub[j, inner] for j in range(8)]
        half = lax.bitwise_and(s, 1)

        @pl.when(s >= 2)
        def _():
            leave(s - 2).wait()

        z = z_neighbours(second)
        low, top = y_neighbours(second, ghost)
        for j in range(8):
            both = ua[j, inner] + second[j]
            value = change(j, ub, second[j], low, top, z)
            uc[j] = value
            fbuf[half, :, 128 * j : 128 * j + 128] = value
            zr[j] = fb[j] * both - 2.0 * gc[j]
            for at, row, out_row in ((0, 8, 0), (32, 39, W - 1)):
                outer = 7 if row == 8 else 40
                total = ua[j, row : row + 1] + ub[j, row : row + 1] - 2.0 * ua[j, outer : outer + 1]
                b1[j, s, out_row : out_row + 1] = fx[j, at : at + 1] * total
            if j == 0:
                yr[...] = jnp.where(lane32 < 32, fyl[0] * (both - 2.0 * ghost), 0.0)
            if j == 7:
                yr[...] = jnp.where(lane32 < 96, yr[...], fyh[7] * (both - 2.0 * ghost))
        for j in range(8):
            b1[j, s, 1 : CX + 1] = uc[j, pl.ds(0, CX, stride=2), :] + uc[j, pl.ds(1, CX, stride=2), :]
            b2[j, s, 1 : CX + 1] = zr[j, pl.ds(0, CX, stride=2), :] + zr[j, pl.ds(1, CX, stride=2), :]
        by[s, 1 : CX + 1] = yr[pl.ds(0, CX, stride=2), :] + yr[pl.ds(1, CX, stride=2), :]
        leave(s).start()
        return carry

    lax.fori_loop(0, S, species, 0)

    lane_out = lanes((CH * PITCH, 128))
    delta = [jnp.zeros((CH * PITCH, 128), F32) for _ in range(3)]
    for j in range(8):
        t, off = divmod(2 * W * j + W, 128)
        sums = spread(b1[j].reshape(CH * PITCH, 128), tabs[:, 896:1024])
        sums = pltpu.roll(sums + spread(b2[j].reshape(CH * PITCH, 128), tabs[:, 1024:1152]), off, 1)
        if off + 2 * W > 128:
            delta[t] = delta[t] + jnp.where(lane_out >= off, sums, 0.0)
            delta[t + 1] = delta[t + 1] + jnp.where(lane_out < off, sums, 0.0)
        else:
            delta[t] = delta[t] + sums
    sums = spread(by[...].reshape(CH * PITCH, 128), tabs[:, 768:896])
    delta[0] = delta[0] + jnp.where(lane_out < W, sums, 0.0)
    delta[2] = delta[2] + jnp.where(lane_out >= 50, sums, 0.0)
    for t in range(3):
        dl[t] = delta[t].reshape(CH, PITCH, 128)

    rows3 = 3 * PITCH
    lane_c = lanes((rows3, 128))
    lane24 = lanes((PITCH, 128))
    row24 = lax.broadcasted_iota(jnp.int32, (PITCH, 128), 0)

    def within(a, top):
        return jnp.logical_and(a >= 1, a <= top)

    def shifted_down(tiles, by_lanes):
        moved = [pltpu.roll(a, by_lanes, 1) for a in tiles]
        return [jnp.where(lane_c < by_lanes, moved[t - 1], moved[t]) for t in range(3)]

    def shifted_up(tiles, by_lanes):
        moved = [pltpu.roll(a, 128 - by_lanes, 1) for a in tiles]
        return [jnp.where(lane_c < 128 - by_lanes, moved[t], moved[(t + 1) % 3]) for t in range(3)]

    for t in range(3):
        cell = lane24 + 128 * t
        y = lax.shift_right_logical(cell * 3641, 16)
        z = cell - W * y
        inside = [within(row24, CX), within(y, CX), within(z, CX)]
        wider = [within(row24, CX + 1), within(y, CX + 1), within(z, CX + 1)]
        every = lambda a, b, c: jnp.logical_and(a, jnp.logical_and(b, c))
        faces = [every(*(wider[n] if n == axis else inside[n] for n in range(3))) for axis in range(3)]
        for i in range(3):
            for axis in range(3):
                mk[3 * axis + t, 24 * i : 24 * i + 24] = jnp.where(faces[axis], 0.5, 0.0)
            mk[9 + t, 24 * i : 24 * i + 24] = jnp.where(every(*inside), 1.0, 0.0)

    def coarse(i, carry):
        u = [fr[t, pl.ds(3 * i, 3)].reshape(rows3, 128) for t in range(3)]
        d = [fr[t, pl.ds(S + 3 * i, 3)].reshape(rows3, 128) for t in range(3)]
        below = [[pltpu.roll(a, 1, 0) for a in v] for v in (u, d)]
        flux = [[mk[t] * (d[t] + below[1][t]) * (u[t] - below[0][t]) for t in range(3)]]
        for axis, step in ((1, W), (2, 1)):
            down = [shifted_down(v, step) for v in (u, d)]
            flux.append([mk[3 * axis + t] * (d[t] + down[1][t]) * (u[t] - down[0][t]) for t in range(3)])
        up_y, up_z = shifted_up(flux[1], W), shifted_up(flux[2], 1)
        for t in range(3):
            total = pltpu.roll(flux[0][t], rows3 - 1, 0) - flux[0][t]
            total = total + (up_y[t] - flux[1][t]) + (up_z[t] - flux[2][t])
            old = dl[t, pl.ds(3 * i, 3)].reshape(rows3, 128)
            dl[t, pl.ds(3 * i, 3)] = (old - (mk[9 + t] * u[t] + total)).reshape(3, PITCH, 128)
        return carry

    lax.fori_loop(0, S // 3, coarse, 0)

    for t in range(3):
        hb[t, 16:24] = zero8
        for s in range(S):
            hb[t, s : s + 1] = dl[t, s, 0:1]
            hb[t, S + s : S + s + 1] = dl[t, s, W - 1 : W]

    def group_tiles(g):
        if g < 2 * S:
            return [dl[t, g // 2, 1 + 8 * (g % 2) : 9 + 8 * (g % 2)] for t in range(3)]
        return [hb[t, 8 * (g - 2 * S) : 8 * (g - 2 * S) + 8] for t in range(3)]

    main_from = ([0], [0, 1, 2], [1, 2, 3], [2, 3])
    rest_from = ([0, 1], [1, 2], [2, 3], [])

    def send(k):
        return pltpu.make_async_copy(bbuf.at[k], back.at[owner + k], bsem.at[k])

    for k in range(4):

        @pl.when(8 * k - y0 < W)
        def _(k=k):
            rest = None
            for g in range(GB):
                tiles = group_tiles(g) + [None]
                slot = 16 * (g % 8)

                def cut(number, amount, at):
                    value = zero8
                    for t in number:
                        piece = zero8 if tiles[t] is None else pltpu.roll(tiles[t], mod128(amount), 1)
                        value = jnp.where(lane >= 128 * t - at, piece, value)
                    return value

                bbuf[k, g] = cut(main_from[k], 512 - start[k], start[k])
                part = cut(rest_from[k], 512 - start[k] + slot, start[k] + 128 - slot)
                rest = part if slot == 0 else jnp.where(lane >= slot, part, rest)
                if slot == 112 or g == GB - 1:
                    bbuf[k, GB + g // 8] = rest
            send(k).start()


    for k in range(4):

        @pl.when(8 * k - y0 < W)
        def _(k=k):
            send(k).wait()

    for s in (S - 2, S - 1):
        leave(jnp.int32(s)).wait()


def add_windows(roots, arrived, acc, groups, stride, first=None):
    grp, me = lax.axis_index("grp"), lax.axis_index("dev")
    lane = lanes((8, 128))

    def clear(i, carry):
        acc[pl.ds(pl.multiple_of(8 * i, 8), 8), :] = jnp.zeros((8, 128), F32)
        return carry

    lax.fori_loop(0, stride, clear, 0)
    if first is not None:
        first()

    def one(p, carry):
        owner, y0, z0 = where_is(roots, grp * DEV + p)

        @pl.when(jnp.logical_and(me >= owner, 8 * (me - owner) - y0 < W))
        def _():
            window = jnp.logical_and(lane >= z0, lane < z0 + W)
            for number, g in enumerate(groups):
                main, rest = arrived[p, g], arrived[p, GB + g // 8]
                for y in range(8):
                    moved = pltpu.roll(main, mod128(z0 + 128 - W * y), 1)
                    if y == 7:
                        tail = pltpu.roll(rest, mod128(z0 + 2 + 128 - 16 * (g % 8)), 1)
                        moved = jnp.where(lane < z0 + 2, moved, tail)
                    rows = slice(y * stride + 8 * number, y * stride + 8 * number + 8)
                    acc[rows, :] = acc[rows, :] + jnp.where(window, moved, 0.0)

        return carry

    lax.fori_loop(0, DEV, one, 0)


def halo_kernel(roots, arrived, _, low, top, acc):
    add_windows(roots, arrived, acc, range(2 * S, GB), 24)
    for s in range(S):
        low[s] = acc[pl.ds(s, 8, stride=24), :]
        top[s] = acc[pl.ds(S + s, 8, stride=24), :]


def add_kernel(roots, arrived, coarse_one, below, above, own_lo, own_hi, ylo, yhi, ptab, out, acc):
    def faces():
        for at, own, other in ((0, own_lo, ylo), (7 * S * CX, own_hi, yhi)):
            pair = own[S].astype(jnp.int32) * CLS + other[S].astype(jnp.int32)
            for s in range(S):
                tab = jnp.broadcast_to(0.5 * ptab[s : s + 1, :], (8, 128))
                acc[at + s * CX : at + s * CX + CX, :] = pick(tab, pair) * (other[s] - own[s])

    add_windows(roots, arrived, acc, range(2 * S), S * CX, faces)
    for s in range(S):
        for x in range(CX):
            value = coarse_one[s, x] + acc[pl.ds(s * CX + x, 8, stride=S * CX), :]
            if x == 0:
                value = value + below[s]
            if x == CX - 1:
                value = value + above[s]
            out[s, x] = value


def call(kernel, outs, ins, scratch, name, mib, to=VMEM):
    return pl.pallas_call(
        kernel,
        out_shape=outs,
        in_specs=ins,
        out_specs=jax.tree.map(lambda _: to, outs),
        scratch_shapes=scratch,
        compiler_params=pltpu.CompilerParams(vmem_limit_bytes=mib * 1024 * 1024),
        name=name,
    )


def shape(*dims):
    return jax.ShapeDtypeStruct(dims, F32)


def body(coarse_state, coef_index, coef_table, patch_root, fine_index):
    ends_g, ends_d = lax.axis_size("grp") - 1, lax.axis_size("dev") - 1
    up_g, down_g = [(i, i + 1) for i in range(ends_g)], [(i + 1, i) for i in range(ends_g)]
    up_d, down_d = [(i, i + 1) for i in range(ends_d)], [(i + 1, i) for i in range(ends_d)]
    known = jnp.concatenate([jnp.zeros((1, S), F32), coef_table], 0)
    pairs = (0.08 * (known[:, None] + known[None, :])).reshape(CLS * CLS, S)
    ptab = jnp.pad(pairs.T, ((0, 0), (0, 128 - CLS * CLS)))

    def plane(u, c):
        return jnp.concatenate([u, (c[None] + 1).astype(F32)], 0)

    x_lo = lax.ppermute(plane(coarse_state[:, CX - 1], coef_index[CX - 1]), "grp", up_g)
    x_hi = lax.ppermute(plane(coarse_state[:, 0], coef_index[0]), "grp", down_g)
    own_lo = plane(coarse_state[:, :, 0], coef_index[:, 0])
    own_hi = plane(coarse_state[:, :, CY - 1], coef_index[:, CY - 1])
    y_lo = lax.ppermute(own_hi, "dev", up_d)
    y_hi = lax.ppermute(own_lo, "dev", down_d)

    slab = call(
        slab_kernel,
        shape(CY * CH * CX, 128),
        [ANY] * 2,
        [
            pltpu.VMEM((S, CX, CY, 128), F32),
            pltpu.VMEM((CX, CY, 128), jnp.int32),
            pltpu.SemaphoreType.DMA((CH,)),
        ],
        "slab",
        8,
    )(coarse_state, coef_index)
    blocks = call(
        pack_kernel, shape(DEV, NF, 8, 128), [SMEM] + [VMEM] * 3, [pltpu.VMEM((8 * 24, 128), F32)], "pack", 8
    )(patch_root, slab, x_lo, x_hi)
    received = lax.all_to_all(blocks, "dev", split_axis=0, concat_axis=0, tiled=True)
    i32 = lambda *dims: pltpu.VMEM(dims, jnp.int32)
    f32 = lambda *dims: pltpu.VMEM(dims, F32)
    fine_state, corrections = call(
        patch_kernel,
        (shape(1, S, 32, 1024), shape(DEV, NB, 8, 128)),
        [SMEM, SMEM] + [VMEM] * 3,
        [
            f32(3, 2 * S, PITCH, 128), f32(3, PITCH, 128), f32(24, 2 * S, PITCH, 128), f32(2 * S, PITCH, 128),
            f32(8, 48, 128), f32(8, 48, 128), f32(8, 48, 128), f32(8, 32, 128),
            f32(32, 128), f32(32, 128), f32(8, 32, 128), f32(8, 32, 128),
            f32(8, 40, 128), f32(8, 32, 128), f32(8, 32, 128), f32(8, 32, 128), f32(8, 32, 128),
            f32(8, 32, 128), f32(8, 32, 128), f32(8, 32, 128), f32(8, 32, 128), f32(32, 128),
            f32(8, CH, PITCH, 128), f32(8, CH, PITCH, 128), f32(CH, PITCH, 128),
            f32(3, CH, PITCH, 128), f32(12, 3 * PITCH, 128), f32(3, 24, 128),
            f32(2, 32, 1024), f32(4, NB, 8, 128), pltpu.SemaphoreType.DMA((2,)), pltpu.SemaphoreType.DMA((4,)),
        ],
        "patch",
        32,
        ANY,
    )(patch_root, coef_table, received, fine_index, jnp.asarray(weights()))
    arrived = lax.all_to_all(corrections, "dev", split_axis=0, concat_axis=0, tiled=True)
    coarse_one = call(
        coarse_kernel,
        shape(S, CX, CY, 128),
        [VMEM] * 5 + [ANY],
        [i32(CX + 2, 8, 128), i32(CX + 1, 8, 128)] + [i32(CX, 8, 128)] * 4,
        "coarse",
        8,
    )(coarse_state, coef_index, x_lo, x_hi, ptab, corrections)
    low, top = call(
        halo_kernel, (shape(S, CY, 128), shape(S, CY, 128)), [SMEM, VMEM, ANY], [f32(8 * 24, 128)], "halo", 8
    )(patch_root, arrived, coarse_one)
    from_above = lax.ppermute(low, "grp", down_g)
    from_below = lax.ppermute(top, "grp", up_g)
    coarse_new = call(
        add_kernel, shape(S, CX, CY, 128), [SMEM] + [VMEM] * 9, [f32(8 * S * CX, 128)], "add", 8
    )(patch_root, arrived, coarse_one, from_below, from_above, own_lo, own_hi, y_lo, y_hi, ptab)
    return coarse_new, fine_state


def solution(mesh):
    return jax.shard_map(
        body,
        mesh=mesh,
        in_specs=(
            P(None, "grp", "dev", None),
            P("grp", "dev", None),
            P(),
            P(),
            P(("grp", "dev"), None, None),
        ),
        out_specs=(P(None, "grp", "dev", None), P(("grp", "dev"), None, None, None)),
        check_vma=False,
    )
```

```python
import jax
import jax.numpy as jnp
import ml_dtypes
import numpy as np
from jax import lax
from jax.experimental import pallas as pl
from jax.experimental.pallas import tpu as pltpu
from jax.sharding import PartitionSpec as P

F32 = jnp.float32
S = 9
CH = 10
CX = 16
CY = 8
DEV = 16
W = 18
PITCH = 24
FRAME = W * W
BLK = CY * W
GF = 23
NF = GF + 3
GB = 21
NB = GB + 3
CLS = 9
VMEM = pl.BlockSpec(memory_space=pltpu.VMEM)
SMEM = pl.BlockSpec(memory_space=pltpu.SMEM)
ANY = pl.BlockSpec(memory_space=pl.ANY)


def weights():
    wf = np.zeros((128, 384), np.float32)
    rb = np.zeros((2, 128, 128), np.float32)
    for lane in range(128):
        q, fz = divmod(lane, 32)
        k, z = 1 + q // 2, fz // 2 + 1
        sy, sz = (0.125 if q % 2 else -0.125), (0.125 if fz % 2 else -0.125)
        wf[k * W + z, lane] += 1.0
        wf[(k + 1) * W + z, lane] += sy
        wf[(k - 1) * W + z, lane] -= sy
        wf[k * W + z + 1, lane] += sz
        wf[k * W + z - 1, lane] -= sz
        wf[k * W + z, 256 + lane] = 1.0
        rb[0, lane, (q // 2) * W + z] = 0.125
        if fz == 0:
            wf[k * W, 128 + lane] = 1.0
            rb[1, lane, (q // 2) * W] = 0.125
        if fz == 31:
            wf[k * W + W - 1, 128 + lane] = 1.0
            rb[1, lane, (q // 2) * W + W - 1] = 0.125
    wy = np.zeros((128, 128), np.float32)
    ry = np.zeros((128, 128), np.float32)
    for fz in range(32):
        z = fz // 2 + 1
        wy[z, 96 + fz] = 1.0
        wy[W + z, fz] = 1.0
        ry[fz, z] = 0.125
        ry[96 + fz, 50 + z] = 0.125
    wz = np.zeros((128, 256), np.float32)
    for lane in range(128):
        if lane % 32:
            wz[lane - 1, lane] = 1.0
        if lane % 32 != 31:
            wz[lane + 1, 128 + lane] = 1.0
    twice = lambda m: np.concatenate([m, m], 0).astype(ml_dtypes.bfloat16)
    return twice(np.concatenate([wf, wy, wz, ry, rb[0], rb[1]], 1))


def lanes(shape):
    return lax.broadcasted_iota(jnp.int32, shape, 1)


def mod128(x):
    return lax.bitwise_and(x, 127)


def halves(x):
    hi = x.astype(jnp.bfloat16)
    return hi, (x - hi.astype(F32)).astype(jnp.bfloat16)


def pick(tab, index):
    rows = index.shape[0]
    parts = [
        jnp.take_along_axis(tab, index[r : r + 8], axis=1, mode="promise_in_bounds") for r in range(0, rows, 8)
    ]
    return parts[0] if len(parts) == 1 else jnp.concatenate(parts, 0)


def where_is(roots, row):
    first = roots[row, 1] - 1
    owner = lax.shift_right_logical(first, 3)
    return owner, first - 8 * owner, roots[row, 2] - 1


def slab_kernel(u, idx, slab, ubuf, ibuf, sems):
    copies = [pltpu.make_async_copy(u.at[s], ubuf.at[s], sems.at[s]) for s in range(S)]
    copies.append(pltpu.make_async_copy(idx, ibuf, sems.at[S]))
    for copy in copies:
        copy.start()
    for s in range(S):
        copies[s].wait()
        for x in range(CX):
            slab[pl.ds(s * CX + x, 8, stride=CH * CX), :] = ubuf[s, x]
    copies[S].wait()
    for x in range(CX):
        slab[pl.ds(S * CX + x, 8, stride=CH * CX), :] = (ibuf[x] + 1).astype(F32)


def listed(roots, slab, me, into, row):
    count = jnp.int32(0)
    for p in range(DEV):
        owner, y0, _ = where_is(roots, slab * DEV + p)
        into[row, count] = p
        count = count + touches(owner, y0, me).astype(jnp.int32)
    return count


def pack_kernel(roots, slab, lo, hi, out, halo, mine):
    grp, me = lax.axis_index("grp"), lax.axis_index("dev")
    for c in range(CH):
        halo[pl.ds(c, 8, stride=24), :] = lo[c]
        halo[pl.ds(CH + c, 8, stride=24), :] = hi[c]
    for r in range(2 * CH, 24):
        halo[pl.ds(r, 8, stride=24), :] = jnp.zeros((8, 128), F32)
    lane = lanes((8, 128))

    def one(i, carry):
        p = mine[0, i]
        z0 = where_is(roots, grp * DEV + p)[2]
        rest = None
        for g in range(GF):
            main = None
            for y in range(8):
                if g < 2 * CH:
                    rows = slab[y * CH * CX + 8 * g : y * CH * CX + 8 * g + 8, :]
                else:
                    rows = halo[y * 24 + 8 * (g - 2 * CH) : y * 24 + 8 * (g - 2 * CH) + 8, :]
                moved = pltpu.roll(rows, mod128(W * y + 128 - z0), 1)
                main = moved if y == 0 else jnp.where(lane >= W * y, moved, main)
            out[p, g] = main
            slot = 16 * (g % 8)
            moved = pltpu.roll(rows, mod128(126 + slot + 128 - z0), 1)
            rest = moved if slot == 0 else jnp.where(lane >= slot, moved, rest)
            if slot == 112 or g == GF - 1:
                out[p, GF + g // 8] = rest
        return carry

    lax.fori_loop(0, listed(roots, grp, me, mine, 0), one, 0)


def coarse_kernel(u, idx, lo, hi, ptab, _, out, cls, px, pyl, pyh, pzl, pzh):
    lane = lanes((8, 128))
    sub = lax.broadcasted_iota(jnp.int32, (8, 128), 0)
    cls[0] = lo[S].astype(jnp.int32)
    cls[CX + 1] = hi[S].astype(jnp.int32)
    for x in range(CX):
        cls[x + 1] = idx[x] + 1

    def below_z(a):
        return jnp.where(lane == 0, jnp.zeros_like(a), pltpu.roll(a, 1, 1))

    def above_z(a):
        return jnp.where(lane == 127, jnp.zeros_like(a), pltpu.roll(a, 127, 1))

    for x in range(CX + 1):
        px[x] = cls[x + 1] * CLS + cls[x]
    for x in range(CX):
        c = cls[x + 1]
        pyl[x] = jnp.where(sub == 0, 127, c * CLS + pltpu.roll(c, 1, 0))
        pyh[x] = jnp.where(sub == 7, 127, c * CLS + pltpu.roll(c, 7, 0))
        pzl[x] = c * CLS + below_z(c)
        pzh[x] = c * CLS + above_z(c)

    def species(s, carry):
        tab = jnp.broadcast_to(0.5 * ptab[pl.ds(s, 1), :], (8, 128))
        center = u[s, 0]
        flux = pick(tab, px[0]) * (center - lo[s])
        for x in range(CX):
            after = u[s, x + 1] if x + 1 < CX else hi[s]
            next_flux = pick(tab, px[x + 1]) * (after - center)
            total = next_flux - flux
            total = total + pick(tab, pyl[x]) * (pltpu.roll(center, 1, 0) - center)
            total = total + pick(tab, pyh[x]) * (pltpu.roll(center, 7, 0) - center)
            total = total + pick(tab, pzl[x]) * (below_z(center) - center)
            total = total + pick(tab, pzh[x]) * (above_z(center) - center)
            out[s, x] = center + total
            center, flux = after, next_flux
        return carry

    lax.fori_loop(0, S, species, 0)


def patch_kernel(
    roots, table, recv, fidx, tabs,
    fine, dl, flo, fhi,
    fr, fc, up, upy, da, ua, ub, uc, uy, dy, zg, dz, fx, fyl, fyh, fzl, fzh, fb, fs, gc, zr, yr, b1, b2, by, mk, fbuf, fsem,
):
    grp, me = lax.axis_index("grp"), lax.axis_index("dev")
    owner, y0, _ = where_is(roots, grp * DEV + me)
    lane = lanes((8, 128))
    lane_all = lanes((2 * S * PITCH, 128))
    start = [BLK * k - W * y0 for k in range(4)]
    source = [jnp.minimum(owner + k, DEV - 1) for k in range(4)]
    zero8 = jnp.zeros((8, 128), F32)

    for t in range(3):
        for c in range(S):
            fr[t, c, 16:24] = zero8
        fc[t, 16:24] = zero8
    for g in range(GF):
        slot = 16 * (g % 8)
        main = [pltpu.roll(recv[source[k], g], mod128(start[k] + 256), 1) for k in range(4)]
        rest = [pltpu.roll(recv[source[k], GF + g // 8], mod128(start[k] + 384 - slot), 1) for k in range(3)]

        def over(t, piece, at, below):
            return jnp.where(lane >= at - 128 * t, piece, below)

        tile0 = over(0, main[1], start[1], over(0, rest[0], start[0] + 128, main[0]))
        tile1 = over(1, main[1], start[1], rest[0])
        tile1 = over(1, main[2], start[2], over(1, rest[1], start[1] + 128, tile1))
        tile2 = over(2, main[2], start[2], over(2, rest[1], start[1] + 128, main[1]))
        tile2 = over(2, main[3], start[3], over(2, rest[2], start[2] + 128, tile2))
        tile2 = jnp.where(lane < FRAME - 256, tile2, 0.0)
        for t, tile in enumerate((tile0, tile1, tile2)):
            if g < 2 * S:
                fr[t, g // 2, 1 + 8 * (g % 2) : 9 + 8 * (g % 2)] = tile
            elif g < 2 * CH:
                fc[t, 1 + 8 * (g % 2) : 9 + 8 * (g % 2)] = tile
            else:
                for i in range(8):
                    q = 8 * (g - 2 * CH) + i
                    if q < 2 * CH:
                        at = 0 if q < CH else W - 1
                        if q % CH < S:
                            fr[t, q % CH, at : at + 1] = tile[i : i + 1]
                        else:
                            fc[t, at : at + 1] = tile[i : i + 1]

    for t in range(3):
        for r in range(0, PITCH, 8):
            classes = fc[t, r : r + 8]
            masks = [classes == k + 1.0 for k in range(8)]
            for s in range(S):
                value = zero8
                for k in range(8):
                    value = jnp.where(masks[k], 0.08 * table[k, s], value)
                fr[t, S + s, r : r + 8] = value

    rows_all = 2 * S * PITCH

    def spread(values, weight):
        hi, lo = halves(values)
        return jnp.dot(jnp.concatenate([hi, lo], 1), weight, preferred_element_type=F32)

    for j in range(8):
        t, off = divmod(2 * W * j, 128)
        values = fr[t].reshape(rows_all, 128)
        if off:
            values = pltpu.roll(values, 128 - off, 1)
            if off + 4 * W > 128:
                after = pltpu.roll(fr[t + 1].reshape(rows_all, 128), 128 - off, 1)
                values = jnp.where(lane_all < 128 - off, values, after)
        result = spread(values, tabs[:, 0:384])
        for b in range(3):
            up[3 * j + b] = result[:, 128 * b : 128 * b + 128].reshape(2 * S, PITCH, 128)
    ends = jnp.where(
        lane_all < W,
        pltpu.roll(fr[2].reshape(rows_all, 128), 78, 1),
        pltpu.roll(fr[0].reshape(rows_all, 128), W, 1),
    )
    upy[...] = spread(ends, tabs[:, 384:512]).reshape(2 * S, PITCH, 128)

    for c in range(CH):
        for j in range(8):
            b1[j, c, 16:24] = zero8
            b2[j, c, 0:8] = zero8
            b2[j, c, 16:24] = zero8
            if c == S:
                b1[j, c, 0:8] = zero8
                b1[j, c, 8:16] = zero8
                b2[j, c, 8:16] = zero8
        by[c, 0:8] = zero8
        by[c, 16:24] = zero8
        if c == S:
            by[c, 8:16] = zero8
    for j in range(8):
        da[j, 40:48] = zero8

    lane32 = lanes((32, 128))
    z_low = lax.bitwise_and(lane32, 31) == 0
    z_top = lax.bitwise_and(lane32, 31) == 31
    inner = slice(8, 40)

    def twice(ref, at, values):
        ref[at + (pl.ds(0, CX, stride=2), slice(None))] = values
        ref[at + (pl.ds(1, CX, stride=2), slice(None))] = values

    def z_neighbours(tiles):
        result = spread(jnp.concatenate(tiles, 0), tabs[:, 512:768])
        return [(result[32 * j : 32 * j + 32, :128], result[32 * j : 32 * j + 32, 128:]) for j in range(8)]

    def y_neighbours(tiles, ghost):
        down = [pltpu.roll(a, 32, 1) for a in tiles]
        above = [pltpu.roll(a, 96, 1) for a in tiles]
        low = [jnp.where(lane32 < 32, down[j - 1] if j else ghost, down[j]) for j in range(8)]
        top = [jnp.where(lane32 < 96, above[j], above[j + 1] if j < 7 else ghost) for j in range(8)]
        return low, top

    def change(j, src, u, low, top, z):
        value = fx[j, 0:32] * src[j, 7:39] + fx[j, 1:33] * src[j, 9:41]
        value = value + (fyl[j] * low[j] + fyh[j] * top[j])
        value = value + (fzl[j] * z[j][0] + fzh[j] * z[j][1])
        return u + (value + (gc[j] - fs[j] * u))

    def leave(s):
        half = lax.bitwise_and(s, 1)
        return pltpu.make_async_copy(fbuf.at[half], fine.at[0, s], fsem.at[half])

    def species(s, carry):
        for j in range(8):
            core, dcore = up[3 * j + 2, s], up[3 * j + 2, S + s]
            slope = 0.125 * (up[3 * j + 2, s, 2 : CX + 2] - up[3 * j + 2, s, 0:CX])
            middle = up[3 * j, s, 1 : CX + 1]
            ua[j, pl.ds(8, CX, stride=2), :] = middle - slope
            ua[j, pl.ds(9, CX, stride=2), :] = middle + slope
            for ref, values in ((ua, core), (ub, core), (da, dcore)):
                ref[j, 7:8] = values[0:1]
                ref[j, 40:41] = values[W - 1 : W]
            twice(zg, (j,), up[3 * j + 1, s, 1 : CX + 1])
            twice(dz, (j,), up[3 * j + 1, S + s, 1 : CX + 1])
        twice(uy, (), upy[s, 1 : CX + 1])
        twice(dy, (), upy[S + s, 1 : CX + 1])

        known = [0.08 * table[k, s] for k in range(8)]
        diffs = []
        for j in range(8):
            index = fidx[0, :, 128 * j : 128 * j + 128]
            one, two, four = [lax.bitwise_and(index, bit) != 0 for bit in (1, 2, 4)]
            level = [jnp.where(one, known[k + 1], known[k]) for k in (0, 2, 4, 6)]
            level = [jnp.where(two, level[1], level[0]), jnp.where(two, level[3], level[2])]
            diffs.append(jnp.where(four, level[1], level[0]))
            da[j, inner] = diffs[j]
        z = z_neighbours(diffs)
        low, top = y_neighbours(diffs, dy[...])
        for j in range(8):
            d = diffs[j]
            fx[j] = da[j, 8:48] + da[j, 7:47]
            fyl[j] = d + low[j]
            fyh[j] = d + top[j]
            ghost = dz[j]
            low_z = d + jnp.where(z_low, ghost, z[j][0])
            top_z = d + jnp.where(z_top, ghost, z[j][1])
            fzl[j] = low_z
            fzh[j] = top_z
            edge = jnp.where(z_low, low_z, jnp.where(z_top, top_z, 0.0))
            fb[j] = edge
            gc[j] = edge * zg[j]
            fs[j] = ((fx[j, 0:32] + fx[j, 1:33]) + (fyl[j] + fyh[j])) + (low_z + top_z)

        first = [ua[j, inner] for j in range(8)]
        z = z_neighbours(first)
        ghost = uy[...]
        low, top = y_neighbours(first, ghost)
        for j in range(8):
            ub[j, inner] = change(j, ua, first[j], low, top, z)
        second = [ub[j, inner] for j in range(8)]
        half = lax.bitwise_and(s, 1)

        @pl.when(s >= 2)
        def _():
            leave(s - 2).wait()

        z = z_neighbours(second)
        low, top = y_neighbours(second, ghost)
        for j in range(8):
            both = ua[j, inner] + second[j]
            value = change(j, ub, second[j], low, top, z)
            uc[j] = value
            fbuf[half, :, 128 * j : 128 * j + 128] = value
            zr[j] = fb[j] * both - 2.0 * gc[j]
            for at, row, out_row in ((0, 8, 0), (32, 39, W - 1)):
                outer = 7 if row == 8 else 40
                total = ua[j, row : row + 1] + ub[j, row : row + 1] - 2.0 * ua[j, outer : outer + 1]
                b1[j, s, out_row : out_row + 1] = fx[j, at : at + 1] * total
            if j == 0:
                yr[...] = jnp.where(lane32 < 32, fyl[0] * (both - 2.0 * ghost), 0.0)
            if j == 7:
                yr[...] = jnp.where(lane32 < 96, yr[...], fyh[7] * (both - 2.0 * ghost))
        for j in range(8):
            b1[j, s, 1 : CX + 1] = uc[j, pl.ds(0, CX, stride=2), :] + uc[j, pl.ds(1, CX, stride=2), :]
            b2[j, s, 1 : CX + 1] = zr[j, pl.ds(0, CX, stride=2), :] + zr[j, pl.ds(1, CX, stride=2), :]
        by[s, 1 : CX + 1] = yr[pl.ds(0, CX, stride=2), :] + yr[pl.ds(1, CX, stride=2), :]
        leave(s).start()
        return carry

    lax.fori_loop(0, S, species, 0)

    lane_out = lanes((CH * PITCH, 128))
    delta = [jnp.zeros((CH * PITCH, 128), F32) for _ in range(3)]
    for j in range(8):
        t, off = divmod(2 * W * j + W, 128)
        sums = spread(b1[j].reshape(CH * PITCH, 128), tabs[:, 896:1024])
        sums = pltpu.roll(sums + spread(b2[j].reshape(CH * PITCH, 128), tabs[:, 1024:1152]), off, 1)
        if off + 2 * W > 128:
            delta[t] = delta[t] + jnp.where(lane_out >= off, sums, 0.0)
            delta[t + 1] = delta[t + 1] + jnp.where(lane_out < off, sums, 0.0)
        else:
            delta[t] = delta[t] + sums
    sums = spread(by[...].reshape(CH * PITCH, 128), tabs[:, 768:896])
    delta[0] = delta[0] + jnp.where(lane_out < W, sums, 0.0)
    delta[2] = delta[2] + jnp.where(lane_out >= 50, sums, 0.0)
    for t in range(3):
        dl[t] = delta[t].reshape(CH, PITCH, 128)

    rows3 = 3 * PITCH
    lane_c = lanes((rows3, 128))
    lane24 = lanes((PITCH, 128))
    row24 = lax.broadcasted_iota(jnp.int32, (PITCH, 128), 0)

    def within(a, top):
        return jnp.logical_and(a >= 1, a <= top)

    def shifted_down(tiles, by_lanes):
        moved = [pltpu.roll(a, by_lanes, 1) for a in tiles]
        return [jnp.where(lane_c < by_lanes, moved[t - 1], moved[t]) for t in range(3)]

    def shifted_up(tiles, by_lanes):
        moved = [pltpu.roll(a, 128 - by_lanes, 1) for a in tiles]
        return [jnp.where(lane_c < 128 - by_lanes, moved[t], moved[(t + 1) % 3]) for t in range(3)]

    for t in range(3):
        cell = lane24 + 128 * t
        y = lax.shift_right_logical(cell * 3641, 16)
        z = cell - W * y
        inside = [within(row24, CX), within(y, CX), within(z, CX)]
        wider = [within(row24, CX + 1), within(y, CX + 1), within(z, CX + 1)]
        every = lambda a, b, c: jnp.logical_and(a, jnp.logical_and(b, c))
        faces = [every(*(wider[n] if n == axis else inside[n] for n in range(3))) for axis in range(3)]
        for i in range(3):
            for axis in range(3):
                mk[3 * axis + t, 24 * i : 24 * i + 24] = jnp.where(faces[axis], 0.5, 0.0)
            mk[9 + t, 24 * i : 24 * i + 24] = jnp.where(every(*inside), 1.0, 0.0)

    def coarse(i, carry):
        u = [fr[t, pl.ds(3 * i, 3)].reshape(rows3, 128) for t in range(3)]
        d = [fr[t, pl.ds(S + 3 * i, 3)].reshape(rows3, 128) for t in range(3)]
        below = [[pltpu.roll(a, 1, 0) for a in v] for v in (u, d)]
        flux = [[mk[t] * (d[t] + below[1][t]) * (u[t] - below[0][t]) for t in range(3)]]
        for axis, step in ((1, W), (2, 1)):
            down = [shifted_down(v, step) for v in (u, d)]
            flux.append([mk[3 * axis + t] * (d[t] + down[1][t]) * (u[t] - down[0][t]) for t in range(3)])
        up_y, up_z = shifted_up(flux[1], W), shifted_up(flux[2], 1)
        for t in range(3):
            total = pltpu.roll(flux[0][t], rows3 - 1, 0) - flux[0][t]
            total = total + (up_y[t] - flux[1][t]) + (up_z[t] - flux[2][t])
            old = dl[t, pl.ds(3 * i, 3)].reshape(rows3, 128)
            dl[t, pl.ds(3 * i, 3)] = (old - (mk[9 + t] * u[t] + total)).reshape(3, PITCH, 128)
        return carry

    lax.fori_loop(0, S // 3, coarse, 0)

    for t in range(3):
        for ref, row, last in ((flo, 0, 8), (fhi, W - 1, 9)):
            ref[t, 8:16] = zero8
            for s in range(S):
                at = s if s < 8 else last
                ref[t, at : at + 1] = dl[t, s, row : row + 1]
    for s in (S - 2, S - 1):
        leave(jnp.int32(s)).wait()


def beside(grp, step):
    last = lax.axis_size("grp") - 1
    return (grp < last, jnp.minimum(grp + 1, last)) if step > 0 else (grp > 0, jnp.maximum(grp - 1, 0))


def touches(owner, y0, dev):
    return jnp.logical_and(dev >= owner, 8 * (dev - owner) - y0 < W)


def cut_kernel(roots, dl, above, below, back, buf, sems):
    grp, me = lax.axis_index("grp"), lax.axis_index("dev")
    lane = lanes((8, 128))
    sub = lax.broadcasted_iota(jnp.int32, (8, 128), 0)
    zero8 = jnp.zeros((8, 128), F32)
    main_from = ([0], [0, 1, 2], [1, 2, 3], [2, 3])
    rest_from = ([0, 1], [1, 2], [2, 3], [])

    def cut(tiles, number, amount, at):
        value = zero8
        for t in number:
            piece = zero8 if t == 3 else pltpu.roll(tiles[t], mod128(amount), 1)
            value = jnp.where(lane >= 128 * t - at, piece, value)
        return value

    def parts(tiles, k, y0, slot):
        start = BLK * k - W * y0
        main = cut(tiles, main_from[k], 512 - start, start)
        return main, cut(tiles, rest_from[k], 512 - start + slot, start + 128 - slot)

    def always_or(k, offset):
        return (lambda f: f()) if k < 3 else pl.when(8 * k - offset < W)

    owner, y0, _ = where_is(roots, grp * DEV + me)

    def own_rows(k):
        return [
            pltpu.make_async_copy(
                buf.at[owner + k, first : first + size], back.at[owner + k, first : first + size], sems.at[2 * k + n]
            )
            for n, (first, size) in enumerate(((0, 2 * S), (GB, 2)))
        ]

    for k in range(4):

        @always_or(k, y0)
        def _(k=k):
            to = owner + k
            for g in range(2 * S):
                slot = 16 * (g % 8)
                tiles = [dl[t, g // 2, 1 + 8 * (g % 2) : 9 + 8 * (g % 2)] for t in range(3)]
                buf[to, g], part = parts(tiles, k, y0, slot)
                rest = part if slot == 0 else jnp.where(lane >= slot, part, rest)
                if slot == 112:
                    buf[to, GB + g // 8] = rest
            buf[to, GB + 2] = jnp.where(lane < 32, rest, buf[to, GB + 2])
            for copy in own_rows(k):
                copy.start()

    for step, faces, group, row in ((1, above, 18, 0), (-1, below, 19, 1)):
        near, y_near, _ = where_is(roots, beside(grp, step)[1] * DEV + me)
        for k in range(4):

            @always_or(k, y_near)
            def _(k=k, faces=faces, group=group, row=row, near=near, y_near=y_near):
                to = near + k
                slot = 16 * (group - 16)
                buf[to, group], rest = parts([faces[t, 0:8] for t in range(3)], k, y_near, slot)
                main, last = parts([faces[t, 8:16] for t in range(3)], k, y_near, 64)
                buf[to, 20] = jnp.where(sub == row, main, buf[to, 20])
                own_lanes = jnp.logical_and(lane >= slot, lane < slot + 16)
                last_lanes = jnp.logical_and(jnp.logical_and(lane >= 64, lane < 80), sub == row)
                old = buf[to, GB + 2]
                buf[to, GB + 2] = jnp.where(own_lanes, rest, jnp.where(last_lanes, last, old))

    shared = [
        pltpu.make_async_copy(
            buf.at[:, first : first + size], back.at[:, first : first + size], sems.at[8 + n]
        )
        for n, (first, size) in enumerate(((2 * S, 3), (GB + 2, 1)))
    ]
    for copy in shared:
        copy.start()
    for k in range(4):

        @always_or(k, y0)
        def _(k=k):
            for copy in own_rows(k):
                copy.wait()

    for copy in shared:
        copy.wait()


def add_kernel(roots, arrived, coarse_one, own_lo, own_hi, ylo, yhi, ptab, result, out, acc, acc2, mine, sems):
    def faces():
        for at, own, other in ((0, own_lo, ylo), (7 * S * CX, own_hi, yhi)):
            pair = own[S].astype(jnp.int32) * CLS + other[S].astype(jnp.int32)
            for s in range(S):
                tab = jnp.broadcast_to(0.5 * ptab[s : s + 1, :], (8, 128))
                acc[at + s * CX : at + s * CX + CX, :] = pick(tab, pair) * (other[s] - own[s])

    grp, me = lax.axis_index("grp"), lax.axis_index("dev")
    lane = lanes((8, 128))
    zero8 = jnp.zeros((8, 128), F32)

    def clear(i, carry):
        acc[pl.ds(pl.multiple_of(8 * i, 8), 8), :] = zero8
        return carry

    lax.fori_loop(0, S * CX, clear, 0)
    for i in range(32):
        acc2[8 * i : 8 * i + 8, :] = zero8
    faces()
    jobs = [(jnp.bool_(True), grp, range(2 * S), acc, S * CX, 0)]
    jobs.append(beside(grp, 1) + ((18, 20), acc2, 32, 0))
    jobs.append(beside(grp, -1) + ((19, 20), acc2, 32, 16))

    for number, (there, slab, groups, into, stride, base) in enumerate(jobs):

        def one(i, carry, number=number, slab=slab, groups=groups, into=into, stride=stride, base=base):
            p = mine[number, i]
            z0 = where_is(roots, slab * DEV + p)[2]
            window = jnp.logical_and(lane >= z0, lane < z0 + W)
            for at_group, g in enumerate(groups):
                main, rest = arrived[p, g], arrived[p, GB + g // 8]
                for y in range(8):
                    moved = pltpu.roll(main, mod128(z0 + 128 - W * y), 1)
                    if y == 7:
                        tail = pltpu.roll(rest, mod128(z0 + 2 + 128 - 16 * (g % 8)), 1)
                        moved = jnp.where(lane < z0 + 2, moved, tail)
                    at = y * stride + base + 8 * at_group
                    into[at : at + 8, :] = into[at : at + 8, :] + jnp.where(window, moved, 0.0)
            return carry

        lax.fori_loop(0, jnp.where(there, listed(roots, slab, me, mine, number), 0), one, 0)
    copies = [pltpu.make_async_copy(out.at[s], result.at[s], sems.at[s]) for s in range(S)]
    for s in range(S):
        for x in range(CX):
            value = coarse_one[s, x] + acc[pl.ds(s * CX + x, 8, stride=S * CX), :]
            if x == CX - 1:
                value = value + acc2[pl.ds(s, 8, stride=32), :]
            if x == 0:
                value = value + acc2[pl.ds(16 + s if s < 8 else 25, 8, stride=32), :]
            out[s, x] = value
        copies[s].start()
    for copy in copies:
        copy.wait()


def call(kernel, outs, ins, scratch, name, mib, to=VMEM):
    return pl.pallas_call(
        kernel,
        out_shape=outs,
        in_specs=ins,
        out_specs=to,
        scratch_shapes=scratch,
        compiler_params=pltpu.CompilerParams(vmem_limit_bytes=mib * 1024 * 1024),
        name=name,
    )


def shape(*dims):
    return jax.ShapeDtypeStruct(dims, F32)


def body(coarse_state, coef_index, coef_table, patch_root, fine_index):
    ends_g, ends_d = lax.axis_size("grp") - 1, lax.axis_size("dev") - 1
    up_g, down_g = [(i, i + 1) for i in range(ends_g)], [(i + 1, i) for i in range(ends_g)]
    up_d, down_d = [(i, i + 1) for i in range(ends_d)], [(i + 1, i) for i in range(ends_d)]
    known = jnp.concatenate([jnp.zeros((1, S), F32), coef_table], 0)
    pairs = (0.08 * (known[:, None] + known[None, :])).reshape(CLS * CLS, S)
    ptab = jnp.pad(pairs.T, ((0, 0), (0, 128 - CLS * CLS)))

    def plane(u, c):
        return jnp.concatenate([u, (c[None] + 1).astype(F32)], 0)

    x_lo = lax.ppermute(plane(coarse_state[:, CX - 1], coef_index[CX - 1]), "grp", up_g)
    x_hi = lax.ppermute(plane(coarse_state[:, 0], coef_index[0]), "grp", down_g)
    own_lo = plane(coarse_state[:, :, 0], coef_index[:, 0])
    own_hi = plane(coarse_state[:, :, CY - 1], coef_index[:, CY - 1])
    y_lo = lax.ppermute(own_hi, "dev", up_d)
    y_hi = lax.ppermute(own_lo, "dev", down_d)

    slab = call(
        slab_kernel,
        shape(CY * CH * CX, 128),
        [ANY] * 2,
        [
            pltpu.VMEM((S, CX, CY, 128), F32),
            pltpu.VMEM((CX, CY, 128), jnp.int32),
            pltpu.SemaphoreType.DMA((CH,)),
        ],
        "slab",
        8,
    )(coarse_state, coef_index)
    blocks = call(
        pack_kernel, shape(DEV, NF, 8, 128), [SMEM] + [VMEM] * 3, [pltpu.VMEM((8 * 24, 128), F32), pltpu.SMEM((1, DEV + 1), jnp.int32)], "pack", 8
    )(patch_root, slab, x_lo, x_hi)
    received = lax.all_to_all(blocks, "dev", split_axis=0, concat_axis=0, tiled=True)
    i32 = lambda *dims: pltpu.VMEM(dims, jnp.int32)
    f32 = lambda *dims: pltpu.VMEM(dims, F32)
    fine_state, delta, face_lo, face_hi = call(
        patch_kernel,
        (shape(1, S, 32, 1024), shape(3, CH, PITCH, 128), shape(3, 16, 128), shape(3, 16, 128)),
        [SMEM, SMEM] + [VMEM] * 3,
        [
            f32(3, 2 * S, PITCH, 128), f32(3, PITCH, 128), f32(24, 2 * S, PITCH, 128), f32(2 * S, PITCH, 128),
            f32(8, 48, 128), f32(8, 48, 128), f32(8, 48, 128), f32(8, 32, 128),
            f32(32, 128), f32(32, 128), f32(8, 32, 128), f32(8, 32, 128),
            f32(8, 40, 128), f32(8, 32, 128), f32(8, 32, 128), f32(8, 32, 128), f32(8, 32, 128),
            f32(8, 32, 128), f32(8, 32, 128), f32(8, 32, 128), f32(8, 32, 128), f32(32, 128),
            f32(8, CH, PITCH, 128), f32(8, CH, PITCH, 128), f32(CH, PITCH, 128),
            f32(12, 3 * PITCH, 128), f32(2, 32, 1024), pltpu.SemaphoreType.DMA((2,)),
        ],
        "patch",
        32,
        (ANY, VMEM, VMEM, VMEM),
    )(patch_root, coef_table, received, fine_index, jnp.asarray(weights()))
    from_above = lax.ppermute(face_lo, "grp", down_g)
    from_below = lax.ppermute(face_hi, "grp", up_g)
    corrections = call(
        cut_kernel,
        shape(DEV, NB, 8, 128),
        [SMEM] + [VMEM] * 3,
        [f32(DEV, NB, 8, 128), pltpu.SemaphoreType.DMA((10,))],
        "cut",
        12,
        ANY,
    )(patch_root, delta, from_above, from_below)
    arrived = lax.all_to_all(corrections, "dev", split_axis=0, concat_axis=0, tiled=True)
    coarse_one = call(
        coarse_kernel,
        shape(S, CX, CY, 128),
        [VMEM] * 5 + [ANY],
        [i32(CX + 2, 8, 128), i32(CX + 1, 8, 128)] + [i32(CX, 8, 128)] * 4,
        "coarse",
        8,
    )(coarse_state, coef_index, x_lo, x_hi, ptab, corrections)
    coarse_new = call(
        add_kernel,
        shape(S, CX, CY, 128),
        [SMEM] + [VMEM] * 7,
        [
            f32(S, CX, CY, 128),
            f32(8 * S * CX, 128),
            f32(8 * 32, 128),
            pltpu.SMEM((3, DEV + 1), jnp.int32),
            pltpu.SemaphoreType.DMA((S,)),
        ],
        "add",
        8,
        ANY,
    )(patch_root, arrived, coarse_one, own_lo, own_hi, y_lo, y_hi, ptab)
    return coarse_new, fine_state


def solution(mesh):
    return jax.shard_map(
        body,
        mesh=mesh,
        in_specs=(
            P(None, "grp", "dev", None),
            P("grp", "dev", None),
            P(),
            P(),
            P(("grp", "dev"), None, None),
        ),
        out_specs=(P(None, "grp", "dev", None), P(("grp", "dev"), None, None, None)),
        check_vma=False,
    )
```

```python
import jax
import jax.numpy as jnp
import ml_dtypes
import numpy as np
from jax import lax
from jax.experimental import pallas as pl
from jax.experimental.pallas import tpu as pltpu
from jax.sharding import PartitionSpec as P

F32 = jnp.float32
S = 9
CH = 10
CX = 16
CY = 8
DEV = 16
W = 18
PITCH = 24
FRAME = W * W
BLK = CY * W
GF = 23
NF = GF + 3
GB = 21
NB = GB + 3
CLS = 9
VMEM = pl.BlockSpec(memory_space=pltpu.VMEM)
SMEM = pl.BlockSpec(memory_space=pltpu.SMEM)
ANY = pl.BlockSpec(memory_space=pl.ANY)


def weights():
    wf = np.zeros((128, 384), np.float32)
    rb = np.zeros((2, 128, 128), np.float32)
    for lane in range(128):
        q, fz = divmod(lane, 32)
        k, z = 1 + q // 2, fz // 2 + 1
        sy, sz = (0.125 if q % 2 else -0.125), (0.125 if fz % 2 else -0.125)
        wf[k * W + z, lane] += 1.0
        wf[(k + 1) * W + z, lane] += sy
        wf[(k - 1) * W + z, lane] -= sy
        wf[k * W + z + 1, lane] += sz
        wf[k * W + z - 1, lane] -= sz
        wf[k * W + z, 256 + lane] = 1.0
        rb[0, lane, (q // 2) * W + z] = 0.125
        if fz == 0:
            wf[k * W, 128 + lane] = 1.0
            rb[1, lane, (q // 2) * W] = 0.125
        if fz == 31:
            wf[k * W + W - 1, 128 + lane] = 1.0
            rb[1, lane, (q // 2) * W + W - 1] = 0.125
    wy = np.zeros((128, 128), np.float32)
    ry = np.zeros((128, 128), np.float32)
    for fz in range(32):
        z = fz // 2 + 1
        wy[z, 96 + fz] = 1.0
        wy[W + z, fz] = 1.0
        ry[fz, z] = 0.125
        ry[96 + fz, 50 + z] = 0.125
    wz = np.zeros((128, 256), np.float32)
    for lane in range(128):
        if lane % 32:
            wz[lane - 1, lane] = 1.0
        if lane % 32 != 31:
            wz[lane + 1, 128 + lane] = 1.0
    twice = lambda m: np.concatenate([m, m], 0).astype(ml_dtypes.bfloat16)
    return twice(np.concatenate([wf, wy, wz, ry, rb[0], rb[1]], 1))


def lanes(shape):
    return lax.broadcasted_iota(jnp.int32, shape, 1)


def mod128(x):
    return lax.bitwise_and(x, 127)


def halves(x):
    hi = x.astype(jnp.bfloat16)
    return hi, (x - hi.astype(F32)).astype(jnp.bfloat16)


def pick(tab, index):
    rows = index.shape[0]
    parts = [
        jnp.take_along_axis(tab, index[r : r + 8], axis=1, mode="promise_in_bounds") for r in range(0, rows, 8)
    ]
    return parts[0] if len(parts) == 1 else jnp.concatenate(parts, 0)


def where_is(roots, row):
    first = roots[row, 1] - 1
    owner = lax.shift_right_logical(first, 3)
    return owner, first - 8 * owner, roots[row, 2] - 1


def slab_kernel(u, idx, slab):
    for x in range(CX):
        for s in range(S):
            slab[pl.ds(s * CX + x, 8, stride=CH * CX), :] = u[s, x]
        slab[pl.ds(S * CX + x, 8, stride=CH * CX), :] = (idx[x] + 1).astype(F32)


def listed(roots, slab, me, into, row):
    count = jnp.int32(0)
    for p in range(DEV):
        owner, y0, _ = where_is(roots, slab * DEV + p)
        into[row, count] = p
        count = count + touches(owner, y0, me).astype(jnp.int32)
    return count


def pack_kernel(roots, slab, lo, hi, out, halo, mine):
    grp, me = lax.axis_index("grp"), lax.axis_index("dev")
    for c in range(CH):
        halo[pl.ds(c, 8, stride=24), :] = lo[c]
        halo[pl.ds(CH + c, 8, stride=24), :] = hi[c]
    for r in range(2 * CH, 24):
        halo[pl.ds(r, 8, stride=24), :] = jnp.zeros((8, 128), F32)
    lane = lanes((8, 128))

    def one(i, carry):
        p = mine[0, i]
        z0 = where_is(roots, grp * DEV + p)[2]
        rest = None
        for g in range(GF):
            main = None
            for y in range(8):
                if g < 2 * CH:
                    rows = slab[y * CH * CX + 8 * g : y * CH * CX + 8 * g + 8, :]
                else:
                    rows = halo[y * 24 + 8 * (g - 2 * CH) : y * 24 + 8 * (g - 2 * CH) + 8, :]
                moved = pltpu.roll(rows, mod128(W * y + 128 - z0), 1)
                main = moved if y == 0 else jnp.where(lane >= W * y, moved, main)
            out[p, g] = main
            slot = 16 * (g % 8)
            moved = pltpu.roll(rows, mod128(126 + slot + 128 - z0), 1)
            rest = moved if slot == 0 else jnp.where(lane >= slot, moved, rest)
            if slot == 112 or g == GF - 1:
                out[p, GF + g // 8] = rest
        return carry

    lax.fori_loop(0, listed(roots, grp, me, mine, 0), one, 0)


def coarse_kernel(u, idx, lo, hi, ptab, _, out, cls, px, pyl, pyh, pzl, pzh):
    lane = lanes((8, 128))
    sub = lax.broadcasted_iota(jnp.int32, (8, 128), 0)
    cls[0] = lo[S].astype(jnp.int32)
    cls[CX + 1] = hi[S].astype(jnp.int32)
    for x in range(CX):
        cls[x + 1] = idx[x] + 1

    def below_z(a):
        return jnp.where(lane == 0, jnp.zeros_like(a), pltpu.roll(a, 1, 1))

    def above_z(a):
        return jnp.where(lane == 127, jnp.zeros_like(a), pltpu.roll(a, 127, 1))

    for x in range(CX + 1):
        px[x] = cls[x + 1] * CLS + cls[x]
    for x in range(CX):
        c = cls[x + 1]
        pyl[x] = jnp.where(sub == 0, 127, c * CLS + pltpu.roll(c, 1, 0))
        pyh[x] = jnp.where(sub == 7, 127, c * CLS + pltpu.roll(c, 7, 0))
        pzl[x] = c * CLS + below_z(c)
        pzh[x] = c * CLS + above_z(c)

    def species(s, carry):
        tab = jnp.broadcast_to(0.5 * ptab[pl.ds(s, 1), :], (8, 128))
        center = u[s, 0]
        flux = pick(tab, px[0]) * (center - lo[s])
        for x in range(CX):
            after = u[s, x + 1] if x + 1 < CX else hi[s]
            next_flux = pick(tab, px[x + 1]) * (after - center)
            total = next_flux - flux
            total = total + pick(tab, pyl[x]) * (pltpu.roll(center, 1, 0) - center)
            total = total + pick(tab, pyh[x]) * (pltpu.roll(center, 7, 0) - center)
            total = total + pick(tab, pzl[x]) * (below_z(center) - center)
            total = total + pick(tab, pzh[x]) * (above_z(center) - center)
            out[s, x] = center + total
            center, flux = after, next_flux
        return carry

    lax.fori_loop(0, S, species, 0)


def patch_kernel(
    roots, table, recv, fidx, tabs,
    fine, dl, flo, fhi,
    fr, fc, up, upy, da, ua, ub, uc, uy, dy, zg, dz, fx, fyl, fyh, fzl, fzh, fb, fs, gc, zr, yr, b1, b2, by, mk, fbuf, fsem,
):
    grp, me = lax.axis_index("grp"), lax.axis_index("dev")
    owner, y0, _ = where_is(roots, grp * DEV + me)
    lane = lanes((8, 128))
    lane_all = lanes((2 * S * PITCH, 128))
    start = [BLK * k - W * y0 for k in range(4)]
    source = [jnp.minimum(owner + k, DEV - 1) for k in range(4)]
    zero8 = jnp.zeros((8, 128), F32)

    for t in range(3):
        for c in range(S):
            fr[t, c, 16:24] = zero8
        fc[t, 16:24] = zero8
    for g in range(GF):
        slot = 16 * (g % 8)
        main = [pltpu.roll(recv[source[k], g], mod128(start[k] + 256), 1) for k in range(4)]
        rest = [pltpu.roll(recv[source[k], GF + g // 8], mod128(start[k] + 384 - slot), 1) for k in range(3)]

        def over(t, piece, at, below):
            return jnp.where(lane >= at - 128 * t, piece, below)

        tile0 = over(0, main[1], start[1], over(0, rest[0], start[0] + 128, main[0]))
        tile1 = over(1, main[1], start[1], rest[0])
        tile1 = over(1, main[2], start[2], over(1, rest[1], start[1] + 128, tile1))
        tile2 = over(2, main[2], start[2], over(2, rest[1], start[1] + 128, main[1]))
        tile2 = over(2, main[3], start[3], over(2, rest[2], start[2] + 128, tile2))
        tile2 = jnp.where(lane < FRAME - 256, tile2, 0.0)
        for t, tile in enumerate((tile0, tile1, tile2)):
            if g < 2 * S:
                fr[t, g // 2, 1 + 8 * (g % 2) : 9 + 8 * (g % 2)] = tile
            elif g < 2 * CH:
                fc[t, 1 + 8 * (g % 2) : 9 + 8 * (g % 2)] = tile
            else:
                for i in range(8):
                    q = 8 * (g - 2 * CH) + i
                    if q < 2 * CH:
                        at = 0 if q < CH else W - 1
                        if q % CH < S:
                            fr[t, q % CH, at : at + 1] = tile[i : i + 1]
                        else:
                            fc[t, at : at + 1] = tile[i : i + 1]

    for t in range(3):
        for r in range(0, PITCH, 8):
            classes = fc[t, r : r + 8]
            masks = [classes == k + 1.0 for k in range(8)]
            for s in range(S):
                value = zero8
                for k in range(8):
                    value = jnp.where(masks[k], 0.08 * table[k, s], value)
                fr[t, S + s, r : r + 8] = value

    rows_all = 2 * S * PITCH

    def spread(values, weight):
        hi, lo = halves(values)
        return jnp.dot(jnp.concatenate([hi, lo], 1), weight, preferred_element_type=F32)

    for j in range(8):
        t, off = divmod(2 * W * j, 128)
        values = fr[t].reshape(rows_all, 128)
        if off:
            values = pltpu.roll(values, 128 - off, 1)
            if off + 4 * W > 128:
                after = pltpu.roll(fr[t + 1].reshape(rows_all, 128), 128 - off, 1)
                values = jnp.where(lane_all < 128 - off, values, after)
        result = spread(values, tabs[:, 0:384])
        for b in range(3):
            up[3 * j + b] = result[:, 128 * b : 128 * b + 128].reshape(2 * S, PITCH, 128)
    ends = jnp.where(
        lane_all < W,
        pltpu.roll(fr[2].reshape(rows_all, 128), 78, 1),
        pltpu.roll(fr[0].reshape(rows_all, 128), W, 1),
    )
    upy[...] = spread(ends, tabs[:, 384:512]).reshape(2 * S, PITCH, 128)

    for c in range(CH):
        for j in range(8):
            b1[j, c, 16:24] = zero8
            b2[j, c, 0:8] = zero8
            b2[j, c, 16:24] = zero8
            if c == S:
                b1[j, c, 0:8] = zero8
                b1[j, c, 8:16] = zero8
                b2[j, c, 8:16] = zero8
        by[c, 0:8] = zero8
        by[c, 16:24] = zero8
        if c == S:
            by[c, 8:16] = zero8
    for j in range(8):
        da[j, 40:48] = zero8

    lane32 = lanes((32, 128))
    z_low = lax.bitwise_and(lane32, 31) == 0
    z_top = lax.bitwise_and(lane32, 31) == 31
    inner = slice(8, 40)

    def twice(ref, at, values):
        ref[at + (pl.ds(0, CX, stride=2), slice(None))] = values
        ref[at + (pl.ds(1, CX, stride=2), slice(None))] = values

    def z_neighbours(tiles):
        result = spread(jnp.concatenate(tiles, 0), tabs[:, 512:768])
        return [(result[32 * j : 32 * j + 32, :128], result[32 * j : 32 * j + 32, 128:]) for j in range(8)]

    def y_neighbours(tiles, ghost):
        down = [pltpu.roll(a, 32, 1) for a in tiles]
        above = [pltpu.roll(a, 96, 1) for a in tiles]
        low = [jnp.where(lane32 < 32, down[j - 1] if j else ghost, down[j]) for j in range(8)]
        top = [jnp.where(lane32 < 96, above[j], above[j + 1] if j < 7 else ghost) for j in range(8)]
        return low, top

    def change(j, src, u, low, top, z):
        value = fx[j, 0:32] * src[j, 7:39] + fx[j, 1:33] * src[j, 9:41]
        value = value + (fyl[j] * low[j] + fyh[j] * top[j])
        value = value + (fzl[j] * z[j][0] + fzh[j] * z[j][1])
        return u + (value + (gc[j] - fs[j] * u))

    def leave(s):
        half = lax.bitwise_and(s, 1)
        return pltpu.make_async_copy(fbuf.at[half], fine.at[0, s], fsem.at[half])

    def species(s, carry):
        for j in range(8):
            core, dcore = up[3 * j + 2, s], up[3 * j + 2, S + s]
            slope = 0.125 * (up[3 * j + 2, s, 2 : CX + 2] - up[3 * j + 2, s, 0:CX])
            middle = up[3 * j, s, 1 : CX + 1]
            ua[j, pl.ds(8, CX, stride=2), :] = middle - slope
            ua[j, pl.ds(9, CX, stride=2), :] = middle + slope
            for ref, values in ((ua, core), (ub, core), (da, dcore)):
                ref[j, 7:8] = values[0:1]
                ref[j, 40:41] = values[W - 1 : W]
            twice(zg, (j,), up[3 * j + 1, s, 1 : CX + 1])
            twice(dz, (j,), up[3 * j + 1, S + s, 1 : CX + 1])
        twice(uy, (), upy[s, 1 : CX + 1])
        twice(dy, (), upy[S + s, 1 : CX + 1])

        known = [0.08 * table[k, s] for k in range(8)]
        diffs = []
        for j in range(8):
            index = fidx[0, :, 128 * j : 128 * j + 128]
            one, two, four = [lax.bitwise_and(index, bit) != 0 for bit in (1, 2, 4)]
            level = [jnp.where(one, known[k + 1], known[k]) for k in (0, 2, 4, 6)]
            level = [jnp.where(two, level[1], level[0]), jnp.where(two, level[3], level[2])]
            diffs.append(jnp.where(four, level[1], level[0]))
            da[j, inner] = diffs[j]
        z = z_neighbours(diffs)
        low, top = y_neighbours(diffs, dy[...])
        for j in range(8):
            d = diffs[j]
            fx[j] = da[j, 8:48] + da[j, 7:47]
            fyl[j] = d + low[j]
            fyh[j] = d + top[j]
            ghost = dz[j]
            low_z = d + jnp.where(z_low, ghost, z[j][0])
            top_z = d + jnp.where(z_top, ghost, z[j][1])
            fzl[j] = low_z
            fzh[j] = top_z
            edge = jnp.where(z_low, low_z, jnp.where(z_top, top_z, 0.0))
            fb[j] = edge
            gc[j] = edge * zg[j]
            fs[j] = ((fx[j, 0:32] + fx[j, 1:33]) + (fyl[j] + fyh[j])) + (low_z + top_z)

        first = [ua[j, inner] for j in range(8)]
        z = z_neighbours(first)
        ghost = uy[...]
        low, top = y_neighbours(first, ghost)
        for j in range(8):
            ub[j, inner] = change(j, ua, first[j], low, top, z)
        second = [ub[j, inner] for j in range(8)]
        half = lax.bitwise_and(s, 1)

        @pl.when(s >= 2)
        def _():
            leave(s - 2).wait()

        z = z_neighbours(second)
        low, top = y_neighbours(second, ghost)
        for j in range(8):
            both = ua[j, inner] + second[j]
            value = change(j, ub, second[j], low, top, z)
            uc[j] = value
            fbuf[half, :, 128 * j : 128 * j + 128] = value
            zr[j] = fb[j] * both - 2.0 * gc[j]
            for at, row, out_row in ((0, 8, 0), (32, 39, W - 1)):
                outer = 7 if row == 8 else 40
                total = ua[j, row : row + 1] + ub[j, row : row + 1] - 2.0 * ua[j, outer : outer + 1]
                b1[j, s, out_row : out_row + 1] = fx[j, at : at + 1] * total
            if j == 0:
                yr[...] = jnp.where(lane32 < 32, fyl[0] * (both - 2.0 * ghost), 0.0)
            if j == 7:
                yr[...] = jnp.where(lane32 < 96, yr[...], fyh[7] * (both - 2.0 * ghost))
        for j in range(8):
            b1[j, s, 1 : CX + 1] = uc[j, pl.ds(0, CX, stride=2), :] + uc[j, pl.ds(1, CX, stride=2), :]
            b2[j, s, 1 : CX + 1] = zr[j, pl.ds(0, CX, stride=2), :] + zr[j, pl.ds(1, CX, stride=2), :]
        by[s, 1 : CX + 1] = yr[pl.ds(0, CX, stride=2), :] + yr[pl.ds(1, CX, stride=2), :]
        leave(s).start()
        return carry

    lax.fori_loop(0, S, species, 0)

    lane_out = lanes((CH * PITCH, 128))
    delta = [jnp.zeros((CH * PITCH, 128), F32) for _ in range(3)]
    for j in range(8):
        t, off = divmod(2 * W * j + W, 128)
        sums = spread(b1[j].reshape(CH * PITCH, 128), tabs[:, 896:1024])
        sums = pltpu.roll(sums + spread(b2[j].reshape(CH * PITCH, 128), tabs[:, 1024:1152]), off, 1)
        if off + 2 * W > 128:
            delta[t] = delta[t] + jnp.where(lane_out >= off, sums, 0.0)
            delta[t + 1] = delta[t + 1] + jnp.where(lane_out < off, sums, 0.0)
        else:
            delta[t] = delta[t] + sums
    sums = spread(by[...].reshape(CH * PITCH, 128), tabs[:, 768:896])
    delta[0] = delta[0] + jnp.where(lane_out < W, sums, 0.0)
    delta[2] = delta[2] + jnp.where(lane_out >= 50, sums, 0.0)
    for t in range(3):
        dl[t] = delta[t].reshape(CH, PITCH, 128)

    rows9 = S * PITCH
    lane_c = lanes((rows9, 128))
    lane24 = lanes((PITCH, 128))
    row24 = lax.broadcasted_iota(jnp.int32, (PITCH, 128), 0)

    def within(a, top):
        return jnp.logical_and(a >= 1, a <= top)

    def shifted_down(tiles, by_lanes):
        moved = [pltpu.roll(a, by_lanes, 1) for a in tiles]
        return [jnp.where(lane_c < by_lanes, moved[t - 1], moved[t]) for t in range(3)]

    def shifted_up(tiles, by_lanes):
        moved = [pltpu.roll(a, 128 - by_lanes, 1) for a in tiles]
        return [jnp.where(lane_c < 128 - by_lanes, moved[t], moved[(t + 1) % 3]) for t in range(3)]

    for t in range(3):
        cell = lane24 + 128 * t
        y = lax.shift_right_logical(cell * 3641, 16)
        z = cell - W * y
        inside = [within(row24, CX), within(y, CX), within(z, CX)]
        wider = [within(row24, CX + 1), within(y, CX + 1), within(z, CX + 1)]
        every = lambda a, b, c: jnp.logical_and(a, jnp.logical_and(b, c))
        faces = [every(*(wider[n] if n == axis else inside[n] for n in range(3))) for axis in range(3)]
        for axis in range(3):
            mk[3 * axis + t] = jnp.where(faces[axis], 0.5, 0.0)
        mk[9 + t] = jnp.where(every(*inside), 1.0, 0.0)

    def masks_of(n):
        return jnp.broadcast_to(mk[n][None], (S, PITCH, 128)).reshape(rows9, 128)

    u = [fr[t, 0:S].reshape(rows9, 128) for t in range(3)]
    d = [fr[t, S : 2 * S].reshape(rows9, 128) for t in range(3)]
    below = [[pltpu.roll(a, 1, 0) for a in v] for v in (u, d)]
    flux = [[masks_of(t) * (d[t] + below[1][t]) * (u[t] - below[0][t]) for t in range(3)]]
    for axis, step in ((1, W), (2, 1)):
        down = [shifted_down(v, step) for v in (u, d)]
        flux.append([masks_of(3 * axis + t) * (d[t] + down[1][t]) * (u[t] - down[0][t]) for t in range(3)])
    up_y, up_z = shifted_up(flux[1], W), shifted_up(flux[2], 1)
    for t in range(3):
        total = pltpu.roll(flux[0][t], rows9 - 1, 0) - flux[0][t]
        total = total + (up_y[t] - flux[1][t]) + (up_z[t] - flux[2][t])
        value = dl[t, 0:S].reshape(rows9, 128) - (masks_of(9 + t) * u[t] + total)
        dl[t, 0:S] = value.reshape(S, PITCH, 128)

    for t in range(3):
        for ref, row, last in ((flo, 0, 8), (fhi, W - 1, 9)):
            ref[t, 8:16] = zero8
            for s in range(S):
                at = s if s < 8 else last
                ref[t, at : at + 1] = dl[t, s, row : row + 1]
    for s in (S - 2, S - 1):
        leave(jnp.int32(s)).wait()


def beside(grp, step):
    last = lax.axis_size("grp") - 1
    return (grp < last, jnp.minimum(grp + 1, last)) if step > 0 else (grp > 0, jnp.maximum(grp - 1, 0))


def touches(owner, y0, dev):
    return jnp.logical_and(dev >= owner, 8 * (dev - owner) - y0 < W)


def cut_kernel(roots, dl, above, below, back, buf, sems):
    grp, me = lax.axis_index("grp"), lax.axis_index("dev")
    lane = lanes((8, 128))
    sub = lax.broadcasted_iota(jnp.int32, (8, 128), 0)
    zero8 = jnp.zeros((8, 128), F32)
    main_from = ([0], [0, 1, 2], [1, 2, 3], [2, 3])
    rest_from = ([0, 1], [1, 2], [2, 3], [])

    def cut(tiles, number, amount, at):
        value = zero8
        for t in number:
            piece = zero8 if t == 3 else pltpu.roll(tiles[t], mod128(amount), 1)
            value = jnp.where(lane >= 128 * t - at, piece, value)
        return value

    def parts(tiles, k, y0, slot):
        start = BLK * k - W * y0
        main = cut(tiles, main_from[k], 512 - start, start)
        return main, cut(tiles, rest_from[k], 512 - start + slot, start + 128 - slot)

    def always_or(k, offset):
        return (lambda f: f()) if k < 3 else pl.when(8 * k - offset < W)

    owner, y0, _ = where_is(roots, grp * DEV + me)

    def own_rows(k):
        return [
            pltpu.make_async_copy(
                buf.at[owner + k, first : first + size], back.at[owner + k, first : first + size], sems.at[2 * k + n]
            )
            for n, (first, size) in enumerate(((0, 2 * S), (GB, 2)))
        ]

    for k in range(4):

        @always_or(k, y0)
        def _(k=k):
            to = owner + k
            for g in range(2 * S):
                slot = 16 * (g % 8)
                tiles = [dl[t, g // 2, 1 + 8 * (g % 2) : 9 + 8 * (g % 2)] for t in range(3)]
                buf[to, g], part = parts(tiles, k, y0, slot)
                rest = part if slot == 0 else jnp.where(lane >= slot, part, rest)
                if slot == 112:
                    buf[to, GB + g // 8] = rest
            buf[to, GB + 2] = jnp.where(lane < 32, rest, buf[to, GB + 2])
            for copy in own_rows(k):
                copy.start()

    for step, faces, group, row in ((1, above, 18, 0), (-1, below, 19, 1)):
        near, y_near, _ = where_is(roots, beside(grp, step)[1] * DEV + me)
        for k in range(4):

            @always_or(k, y_near)
            def _(k=k, faces=faces, group=group, row=row, near=near, y_near=y_near):
                to = near + k
                slot = 16 * (group - 16)
                buf[to, group], rest = parts([faces[t, 0:8] for t in range(3)], k, y_near, slot)
                main, last = parts([faces[t, 8:16] for t in range(3)], k, y_near, 64)
                buf[to, 20] = jnp.where(sub == row, main, buf[to, 20])
                own_lanes = jnp.logical_and(lane >= slot, lane < slot + 16)
                last_lanes = jnp.logical_and(jnp.logical_and(lane >= 64, lane < 80), sub == row)
                old = buf[to, GB + 2]
                buf[to, GB + 2] = jnp.where(own_lanes, rest, jnp.where(last_lanes, last, old))

    shared = [
        pltpu.make_async_copy(
            buf.at[:, first : first + size], back.at[:, first : first + size], sems.at[8 + n]
        )
        for n, (first, size) in enumerate(((2 * S, 3), (GB + 2, 1)))
    ]
    for copy in shared:
        copy.start()
    for k in range(4):

        @always_or(k, y0)
        def _(k=k):
            for copy in own_rows(k):
                copy.wait()

    for copy in shared:
        copy.wait()


def add_kernel(roots, arrived, coarse_one, own_lo, own_hi, ylo, yhi, ptab, result, out, acc, acc2, mine, sems):
    def faces():
        for at, own, other in ((0, own_lo, ylo), (7 * S * CX, own_hi, yhi)):
            pair = own[S].astype(jnp.int32) * CLS + other[S].astype(jnp.int32)
            for s in range(S):
                tab = jnp.broadcast_to(0.5 * ptab[s : s + 1, :], (8, 128))
                acc[at + s * CX : at + s * CX + CX, :] = pick(tab, pair) * (other[s] - own[s])

    grp, me = lax.axis_index("grp"), lax.axis_index("dev")
    lane = lanes((8, 128))
    zero8 = jnp.zeros((8, 128), F32)

    def clear(i, carry):
        acc[pl.ds(pl.multiple_of(8 * i, 8), 8), :] = zero8
        return carry

    lax.fori_loop(0, S * CX, clear, 0)
    for i in range(32):
        acc2[8 * i : 8 * i + 8, :] = zero8
    faces()
    jobs = [(jnp.bool_(True), grp, range(2 * S), acc, S * CX, 0)]
    jobs.append(beside(grp, 1) + ((18, 20), acc2, 32, 0))
    jobs.append(beside(grp, -1) + ((19, 20), acc2, 32, 16))

    for number, (there, slab, groups, into, stride, base) in enumerate(jobs):

        def one(i, carry, number=number, slab=slab, groups=groups, into=into, stride=stride, base=base):
            p = mine[number, i]
            z0 = where_is(roots, slab * DEV + p)[2]
            window = jnp.logical_and(lane >= z0, lane < z0 + W)
            for at_group, g in enumerate(groups):
                main, rest = arrived[p, g], arrived[p, GB + g // 8]
                for y in range(8):
                    moved = pltpu.roll(main, mod128(z0 + 128 - W * y), 1)
                    if y == 7:
                        tail = pltpu.roll(rest, mod128(z0 + 2 + 128 - 16 * (g % 8)), 1)
                        moved = jnp.where(lane < z0 + 2, moved, tail)
                    at = y * stride + base + 8 * at_group
                    into[at : at + 8, :] = into[at : at + 8, :] + jnp.where(window, moved, 0.0)
            return carry

        lax.fori_loop(0, jnp.where(there, listed(roots, slab, me, mine, number), 0), one, 0)
    copies = [pltpu.make_async_copy(out.at[s], result.at[s], sems.at[s]) for s in range(S)]
    for s in range(S):
        for x in range(CX):
            value = coarse_one[s, x] + acc[pl.ds(s * CX + x, 8, stride=S * CX), :]
            if x == CX - 1:
                value = value + acc2[pl.ds(s, 8, stride=32), :]
            if x == 0:
                value = value + acc2[pl.ds(16 + s if s < 8 else 25, 8, stride=32), :]
            out[s, x] = value
        copies[s].start()
    for copy in copies:
        copy.wait()


def call(kernel, outs, ins, scratch, name, mib, to=VMEM):
    return pl.pallas_call(
        kernel,
        out_shape=outs,
        in_specs=ins,
        out_specs=to,
        scratch_shapes=scratch,
        compiler_params=pltpu.CompilerParams(vmem_limit_bytes=mib * 1024 * 1024),
        name=name,
    )


def shape(*dims):
    return jax.ShapeDtypeStruct(dims, F32)


def body(coarse_state, coef_index, coef_table, patch_root, fine_index):
    ends_g, ends_d = lax.axis_size("grp") - 1, lax.axis_size("dev") - 1
    up_g, down_g = [(i, i + 1) for i in range(ends_g)], [(i + 1, i) for i in range(ends_g)]
    up_d, down_d = [(i, i + 1) for i in range(ends_d)], [(i + 1, i) for i in range(ends_d)]
    known = jnp.concatenate([jnp.zeros((1, S), F32), coef_table], 0)
    pairs = (0.08 * (known[:, None] + known[None, :])).reshape(CLS * CLS, S)
    ptab = jnp.pad(pairs.T, ((0, 0), (0, 128 - CLS * CLS)))

    def plane(u, c):
        return jnp.concatenate([u, (c[None] + 1).astype(F32)], 0)

    x_lo = lax.ppermute(plane(coarse_state[:, CX - 1], coef_index[CX - 1]), "grp", up_g)
    x_hi = lax.ppermute(plane(coarse_state[:, 0], coef_index[0]), "grp", down_g)
    own_lo = plane(coarse_state[:, :, 0], coef_index[:, 0])
    own_hi = plane(coarse_state[:, :, CY - 1], coef_index[:, CY - 1])
    y_lo = lax.ppermute(own_hi, "dev", up_d)
    y_hi = lax.ppermute(own_lo, "dev", down_d)

    slab = call(slab_kernel, shape(CY * CH * CX, 128), [VMEM] * 2, [], "slab", 8)(coarse_state, coef_index)
    blocks = call(
        pack_kernel, shape(DEV, NF, 8, 128), [SMEM] + [VMEM] * 3, [pltpu.VMEM((8 * 24, 128), F32), pltpu.SMEM((1, DEV + 1), jnp.int32)], "pack", 8
    )(patch_root, slab, x_lo, x_hi)
    received = lax.all_to_all(blocks, "dev", split_axis=0, concat_axis=0, tiled=True)
    i32 = lambda *dims: pltpu.VMEM(dims, jnp.int32)
    f32 = lambda *dims: pltpu.VMEM(dims, F32)
    fine_state, delta, face_lo, face_hi = call(
        patch_kernel,
        (shape(1, S, 32, 1024), shape(3, CH, PITCH, 128), shape(3, 16, 128), shape(3, 16, 128)),
        [SMEM, SMEM] + [VMEM] * 3,
        [
            f32(3, 2 * S, PITCH, 128), f32(3, PITCH, 128), f32(24, 2 * S, PITCH, 128), f32(2 * S, PITCH, 128),
            f32(8, 48, 128), f32(8, 48, 128), f32(8, 48, 128), f32(8, 32, 128),
            f32(32, 128), f32(32, 128), f32(8, 32, 128), f32(8, 32, 128),
            f32(8, 40, 128), f32(8, 32, 128), f32(8, 32, 128), f32(8, 32, 128), f32(8, 32, 128),
            f32(8, 32, 128), f32(8, 32, 128), f32(8, 32, 128), f32(8, 32, 128), f32(32, 128),
            f32(8, CH, PITCH, 128), f32(8, CH, PITCH, 128), f32(CH, PITCH, 128),
            f32(12, PITCH, 128), f32(2, 32, 1024), pltpu.SemaphoreType.DMA((2,)),
        ],
        "patch",
        32,
        (ANY, VMEM, VMEM, VMEM),
    )(patch_root, coef_table, received, fine_index, jnp.asarray(weights()))
    from_above = lax.ppermute(face_lo, "grp", down_g)
    from_below = lax.ppermute(face_hi, "grp", up_g)
    corrections = call(
        cut_kernel,
        shape(DEV, NB, 8, 128),
        [SMEM] + [VMEM] * 3,
        [f32(DEV, NB, 8, 128), pltpu.SemaphoreType.DMA((10,))],
        "cut",
        12,
        ANY,
    )(patch_root, delta, from_above, from_below)
    arrived = lax.all_to_all(corrections, "dev", split_axis=0, concat_axis=0, tiled=True)
    coarse_one = call(
        coarse_kernel,
        shape(S, CX, CY, 128),
        [VMEM] * 5 + [ANY],
        [i32(CX + 2, 8, 128), i32(CX + 1, 8, 128)] + [i32(CX, 8, 128)] * 4,
        "coarse",
        8,
    )(coarse_state, coef_index, x_lo, x_hi, ptab, corrections)
    coarse_new = call(
        add_kernel,
        shape(S, CX, CY, 128),
        [SMEM] + [VMEM] * 7,
        [
            f32(S, CX, CY, 128),
            f32(8 * S * CX, 128),
            f32(8 * 32, 128),
            pltpu.SMEM((3, DEV + 1), jnp.int32),
            pltpu.SemaphoreType.DMA((S,)),
        ],
        "add",
        8,
        ANY,
    )(patch_root, arrived, coarse_one, own_lo, own_hi, y_lo, y_hi, ptab)
    return coarse_new, fine_state


def solution(mesh):
    return jax.shard_map(
        body,
        mesh=mesh,
        in_specs=(
            P(None, "grp", "dev", None),
            P("grp", "dev", None),
            P(),
            P(),
            P(("grp", "dev"), None, None),
        ),
        out_specs=(P(None, "grp", "dev", None), P(("grp", "dev"), None, None, None)),
        check_vma=False,
    )
```
